32 devices in a mesh: ep: 8 (over z, x), tp: 4 (over y, core).
Axes of the slice: x: 2, y: 2, z: 4, core: 2. Of those that a mesh axis runs over, the one named last changes fastest.
Arguments:
- tokens: bfloat16 [1024, 4096], P('ep', 'tp'), may hold values from -6 to 6
- out_grad: bfloat16 [1024, 4096], P('ep', 'tp'), may hold values from -6 to 6
- routes: int32 [1024, 4], P('ep'), may hold values from 0 to 7, all different within a row; in each aligned block of 128 rows (0 to 127, 128 to 255, ...) at most 128 rows name the same one
- probs: bfloat16 [1024, 4], P('ep'), may hold values from 0.019897461 to 0.59765625
- w_in: bfloat16 [8, 2, 1536, 4096], P('ep', None, 'tp'), as said below
- w_out: bfloat16 [8, 1536, 4096], P('ep', 'tp'), as said below
Outputs:
- in_grad: bfloat16 [1024, 4096], P('ep', 'tp')
- grad_in: bfloat16 [8, 2, 1536, 4096], P('ep', None, 'tp')
- grad_out: bfloat16 [8, 1536, 4096], P('ep', 'tp')
The draws below stay inside these ranges and needn't reach their ends.
Inputs may be any that keep to these rules, and one draw needn't show every extreme that they name: `routes`: each token names 4 different copies; within the tokens of one device (aligned blocks of 128 tokens) no copy is named more than 128 times, a bound that some block reaches. `w_in`: copies c and c + 4 hold equal weights. `w_out`: copies c and c + 4 hold equal weights.
All inputs are finite; a program needn't handle non-finite values.
Results may differ from the reference program's by a relative error of at most 0.02.
Values may be sent and summed in bfloat16 or wider, within the bound.
No kernel may reach another device: no remote copies, remote signals or barrier semaphores. Data moves between devices by JAX's collectives and lax.ppermute only.
A program may use at most 128 MiB of HBM per device.

```python
import math
import jax
import jax.numpy as jnp
import numpy as np
from jax import lax

D = 4096
FF = 1536
TOP = 4
TOK_DEV = 128
COPIES = 8
EXPERTS = 4
CAP = 128
TOKENS = 1024
N_EP = 8
N_TP = 4


def draw_w_in(key, part):
    base = jax.random.normal(key, (EXPERTS, 2, FF, D), jnp.float32) * (1.0 / D ** 0.5)
    return jnp.concatenate([base, base], axis=0).astype(jnp.bfloat16)


def draw_w_out(key, part):
    base = jax.random.normal(jax.random.fold_in(key, 7), (EXPERTS, FF, D), jnp.float32) * (1.0 / FF ** 0.5)
    return jnp.concatenate([base, base], axis=0).astype(jnp.bfloat16)


def level_of(rng, extent, cuts, least, largest):
    gain = 1.0
    for dim, blocks in cuts:
        heights = jax.random.uniform(jax.random.fold_in(jax.random.fold_in(rng, 6), dim), (blocks,), jnp.float32, least / len(cuts), largest / len(cuts))
        gain = gain * jnp.repeat(jnp.exp(heights), extent[dim] // blocks).reshape((-1,) + (1,) * (len(extent) - 1 - dim))
    return gain


def deal_out(own_key, own, number, rows, count, top, reach, lean):
    ranking = jax.random.permutation(own_key, count)
    heavy_load, usual = shares(count, rows * top, reach, lean, True), shares(count, rows * top, reach, lean, False)
    places = jnp.arange(count)

    def named(tallies, offset_by):
        used = int((tallies > 0).sum())
        fixed = max(1, used // 4)
        shifted = fixed + (places - fixed + offset_by * (used - fixed)) % max(1, count - fixed)
        return jnp.zeros((count,), jnp.int32).at[ranking[jnp.where(places < fixed, places, shifted)]].set(jnp.asarray(tallies, jnp.int32))

    tallies = jnp.where(number % 4 == 0, named(heavy_load, number // 4), named(usual, number - number // 4 - 1))
    mixed = jax.random.permutation(jax.random.fold_in(own, 3), count)
    giver, receiver = mixed[0:count // 2 * 2:2], mixed[1:count // 2 * 2:2]
    margin = jnp.minimum(tallies[giver] - 1, reach - tallies[receiver]) // 2
    margin = jnp.where((giver == ranking[0]) | (receiver == ranking[0]) | (tallies[receiver] == 0), 0, jnp.maximum(margin, 0))
    shifted = jax.random.randint(jax.random.fold_in(own, 4), (count // 2,), 0, 1 << 20) % (margin + 1)
    tallies = tallies.at[giver].add(-shifted).at[receiver].add(shifted)
    members = jnp.searchsorted(jnp.cumsum(tallies), jnp.arange(rows * top), side="right").astype(jnp.int32)
    listing = members.reshape(top, rows).T
    listing = listing[jax.random.permutation(jax.random.fold_in(own, 1), rows)]
    offset_by = jax.random.randint(jax.random.fold_in(own, 2), (rows, 1), 0, top)
    return jnp.take_along_axis(listing, (jnp.arange(top)[None, :] + offset_by) % top, axis=1)


def shares(number_of, total, most, skew, full):
    loads = [(1 << 20) // math.isqrt(rank ** skew) + 1 for rank in range(1, number_of + 1)]
    largest = most if full else min(most, max(-(-total // number_of), total * loads[0] // sum(loads)))
    least = 1 if total - largest >= number_of - 1 else 0
    given, surplus = [largest] + [least] * (number_of - 1), total - largest - least * (number_of - 1)
    while surplus > 0:
        movable = [i for i in range(1, number_of) if given[i] < largest] or [i for i in range(1, number_of) if given[i] < most]
        whole, budget = sum([loads[i] for i in movable]), surplus
        for i in movable:
            addition = min(most - given[i], max(1, budget * loads[i] // whole), surplus)
            given[i] = given[i] + addition
            surplus = surplus - addition
    return np.array(given)


def bell_draw(stream_key, dims, deviation, most, shards=(), kind=jnp.bfloat16):
    drawn = deviation * jax.random.normal(stream_key, dims, jnp.float32)
    if shards:
        drawn = drawn * level_of(stream_key, dims, shards, -0.22, 0.18)
    return jnp.clip(drawn, -most, most).astype(kind)


def setup_inputs(seed: int = 0) -> dict:
    keys = jax.random.split(jax.random.key(seed), 7)
    tokens = bell_draw(keys[0], (TOKENS, D), 1.0, 6.0, ((0, 8), (1, 4)))
    out_grad = bell_draw(keys[1], (TOKENS, D), 1.0, 6.0, ((0, 8), (1, 4)))
    routes_keys = jax.random.split(jax.random.fold_in(keys[2], 1), TOKENS // TOK_DEV)
    routes_turns = jax.random.permutation(jax.random.fold_in(keys[2], 3), TOKENS // TOK_DEV)
    routes = jax.vmap(lambda own, number: deal_out(jax.random.fold_in(keys[2], 2), own, number, TOK_DEV, COPIES, TOP, CAP, 2))(routes_keys, routes_turns).reshape((TOKENS, TOP))
    probs = jnp.clip(jnp.exp(math.log(0.59765625) - 3.4024236 * jax.random.uniform(keys[3], (TOKENS, TOP), jnp.float32) ** level_of(keys[3], (TOKENS, TOP), ((0, 8),), -0.2, 0.2)), 0.019897461, 0.59765625).astype(jnp.bfloat16)
    w_in = draw_w_in(jax.random.fold_in(keys[6], 71), 0)
    w_out = draw_w_out(jax.random.fold_in(keys[6], 71), 0)
    return {"tokens": tokens, "out_grad": out_grad, "routes": routes, "probs": probs, "w_in": w_in, "w_out": w_out}


def slot_tables(block_routes, copies, cap):
    flat = block_routes.reshape(-1).astype(jnp.int32)
    nrows = flat.shape[0]
    onehot = (flat[:, None] == jnp.arange(copies, dtype=jnp.int32)[None, :]).astype(jnp.int32)
    ranks = jnp.sum((jnp.cumsum(onehot, axis=0) - 1) * onehot, axis=1)
    slot = (flat * cap + ranks).astype(jnp.int32)
    source = jnp.full((copies * cap,), nrows, jnp.int32).at[slot].set(jnp.arange(nrows, dtype=jnp.int32))
    return slot, source


def reference(tokens, out_grad, routes, probs, w_in, w_out):
    nrows = TOK_DEV * TOP
    blocks = routes.reshape(N_EP, TOK_DEV, TOP)
    slots, sources = jax.vmap(lambda b: slot_tables(b, COPIES, CAP))(blocks)
    per_copy_src = sources.reshape(N_EP, COPIES, CAP).transpose(1, 0, 2)
    probs_flat = probs.reshape(N_EP, nrows)
    contract_last = (((1,), (1,)), ((), ()))
    contract_rows = (((0,), (0,)), ((), ()))

    def one_copy(args):
        src, weights_in, weights_out = args
        valid = src < nrows
        local = jnp.minimum(src, nrows - 1).astype(jnp.int32)
        tok = (jnp.arange(N_EP, dtype=jnp.int32)[:, None] * TOK_DEV + local // TOP).astype(jnp.int32)
        scale = jnp.where(valid, jnp.take_along_axis(probs_flat, local, axis=1).astype(jnp.float32), 0.0)
        rows_x = jnp.where(valid[..., None], tokens[tok], jnp.zeros((), jnp.bfloat16)).reshape(N_EP * CAP, D)
        rows_g = (scale[..., None] * out_grad[tok].astype(jnp.float32)).astype(jnp.bfloat16).reshape(N_EP * CAP, D)
        w_gate = weights_in[0]
        w_up = weights_in[1]
        a = lax.dot_general(rows_x, w_gate, contract_last, preferred_element_type=jnp.float32)
        b = lax.dot_general(rows_x, w_up, contract_last, preferred_element_type=jnp.float32)
        sig = jax.nn.sigmoid(a)
        silu = a * sig
        hidden = (silu * b).astype(jnp.bfloat16)
        dh = lax.dot_general(rows_g, weights_out, contract_last, preferred_element_type=jnp.float32)
        da = (dh * b * sig * (1.0 + a * (1.0 - sig))).astype(jnp.bfloat16)
        db = (dh * silu).astype(jnp.bfloat16)
        ffl = FF // N_TP
        da_t = da.astype(jnp.float32).reshape(N_EP * CAP, N_TP, ffl)
        db_t = db.astype(jnp.float32).reshape(N_EP * CAP, N_TP, ffl)
        wg_t = w_gate.astype(jnp.float32).reshape(N_TP, ffl, D)
        wu_t = w_up.astype(jnp.float32).reshape(N_TP, ffl, D)
        parts = jnp.einsum("rtf,tfd->trd", da_t, wg_t) + jnp.einsum("rtf,tfd->trd", db_t, wu_t)
        row_grad = jnp.sum(parts.astype(jnp.bfloat16).astype(jnp.float32), axis=0).astype(jnp.bfloat16)
        own_in = jnp.stack([
            lax.dot_general(da, rows_x, contract_rows, preferred_element_type=jnp.float32),
            lax.dot_general(db, rows_x, contract_rows, preferred_element_type=jnp.float32)]).astype(jnp.bfloat16)
        own_out = lax.dot_general(hidden, rows_g, contract_rows, preferred_element_type=jnp.float32).astype(jnp.bfloat16)
        return row_grad.reshape(N_EP, CAP, D), own_in, own_out

    row_grads, own_in, own_out = lax.map(one_copy, (per_copy_src, w_in, w_out))
    by_source = row_grads.transpose(1, 0, 2, 3).reshape(N_EP, COPIES * CAP, D)
    picked = jnp.take_along_axis(by_source, slots[..., None], axis=1)
    in_grad = jnp.sum(picked.astype(jnp.float32).reshape(N_EP, TOK_DEV, TOP, D), axis=2).astype(jnp.bfloat16).reshape(TOKENS, D)
    grad_in = (own_in.astype(jnp.float32) + jnp.roll(own_in, EXPERTS, axis=0).astype(jnp.float32)).astype(jnp.bfloat16)
    grad_out = (own_out.astype(jnp.float32) + jnp.roll(own_out, EXPERTS, axis=0).astype(jnp.float32)).astype(jnp.bfloat16)
    return in_grad, grad_in, grad_out
```

```python
import functools

import jax
import jax.numpy as jnp
from jax import lax
from jax.experimental import pallas as pl
from jax.experimental.pallas import tpu as pltpu
from jax.sharding import PartitionSpec as P

BF16 = jnp.bfloat16
F32 = jnp.float32
VMEM_LIMIT = 40 * 1024 * 1024
SHRINK = 1.0 / 64.0


def hop(block, axis, bit):
    count = lax.axis_size(axis)
    return lax.ppermute(block, axis, [(i, i ^ bit) for i in range(count)])


def after(value, *others):
    return lax.optimization_barrier((value,) + others)[0] if others else value


def bits_of(number, letter, skip=0):
    return [f"{letter}{i}" for i in range(skip, number.bit_length() - 1)]


class Lanes:
    def __init__(self, depth):
        self.depth = depth
        self.sent = {}

    def send(self, block, bit, *others):
        queue = self.sent.setdefault(bit, [])
        ready = list(others) + queue[-self.depth : len(queue) - self.depth + 1]
        axis = "ep" if bit[0] == "e" else "tp"
        queue.append(hop(after(block, *ready), axis, 1 << int(bit[1:])))
        return queue[-1]


def gather_plan(n_ep, n_tp):
    if (n_ep, n_tp) == (8, 4):
        x, n, f, y = "e0", "e1", "e2", "t1"
        return [
            ((x,), x, 2), ((y,), y, 2), ((n,), n, 2), ((f,), f, 2),
            ((x, y), x, 0), ((x, y), y, 1), ((x, n), x, 2), ((y, n), y, 2),
            ((x, y, n), n, 2), ((n, f), n, 2), ((x, f), x, 2), ((y, f), y, 2),
            ((x, y, f), x, 0), ((x, y, f), y, 1), ((x, y, n, f), n, 2),
            ((x, n, f), x, 2), ((y, n, f), y, 2),
        ]
    bits = bits_of(n_ep, "e") + bits_of(n_tp, "t", 1)
    plan = []
    for i, bit in enumerate(bits):
        for low in range(1 << i):
            below = tuple(b for j, b in enumerate(bits[:i]) if low >> j & 1)
            plan.append((below + (bit,), bit, 2))
    return plan


def name_of(ep, tp):
    names = [f"e{i}" for i in range(ep.bit_length()) if ep >> i & 1]
    names += [f"t{i + 1}" for i in range(tp.bit_length()) if tp >> i & 1]
    return frozenset(names)


def rows_kernel(n_tp, part, t_ref, p_ref, a_ref, b_ref, win_ref, wout_ref, *rest):
    if part:
        dadb_ref, hid_ref, part_ref, xs, gs, wi, wo, acc, sems = rest
    else:
        dadb_ref, hid_ref, xs, gs, wi, wo, acc, sems = rest
    width = xs.shape[2]
    tok = xs.shape[1] // 2
    ffl = hid_ref.shape[0]
    pairs = n_tp // 2
    copies = []
    for d in range(n_tp):
        src = (a_ref, b_ref)[d % 2]
        column = pl.ds(pl.multiple_of((t_ref[0] ^ d) * width, width), width)
        mine = [
            pltpu.make_async_copy(win_ref.at[:, column], wi.at[d], sems.at[d, 0]),
            pltpu.make_async_copy(wout_ref.at[:, column], wo.at[d], sems.at[d, 1]),
        ]
        for j in range(2):
            for k, dst in enumerate((xs, gs)):
                mine.append(
                    pltpu.make_async_copy(
                        src.at[j * pairs + d // 2, k],
                        dst.at[d, pl.ds(j * tok, tok)],
                        sems.at[d, 2 + 2 * j + k],
                    )
                )
        for copy in mine:
            copy.start()
        copies.append(mine)
    last = (((1,), (1,)), ((), ()))
    for d in range(n_tp):
        for copy in copies[d]:
            copy.wait()
        ab = lax.dot_general(wi[d], xs[d], last, preferred_element_type=F32)
        small = gs[d] * jnp.asarray(SHRINK, BF16)
        h = lax.dot_general(wo[d], small, last, preferred_element_type=F32)
        if d == 0:
            acc[pl.ds(0, 2 * ffl)] = ab
            acc[pl.ds(2 * ffl, ffl)] = h
        else:
            acc[pl.ds(0, 2 * ffl)] += ab
            acc[pl.ds(2 * ffl, ffl)] += h
    a = acc[pl.ds(0, ffl)]
    b = acc[pl.ds(ffl, ffl)]
    scale = p_ref[...]
    named = scale > 0.0
    dh = acc[pl.ds(2 * ffl, ffl)] * (scale * (1.0 / SHRINK))
    sig = jax.nn.sigmoid(a)
    silu = a * sig
    da = dh * b * sig * (1.0 + a * (1.0 - sig))
    dadb_ref[pl.ds(0, ffl)] = jnp.where(named, da, 0.0).astype(BF16)
    dadb_ref[pl.ds(ffl, ffl)] = jnp.where(named, dh * silu, 0.0).astype(BF16)
    hid_ref[...] = jnp.where(named, (0.5 * scale) * (silu * b), 0.0).astype(BF16)
    if part:
        rows = dadb_ref[...].T
        for d in range(n_tp):
            out = jnp.dot(rows, wi[d], preferred_element_type=F32).astype(BF16)
            for j in range(2):
                part_ref[d % 2, j * pairs + d // 2] = out[j * tok : (j + 1) * tok]


def rows_call(part, t, p, a, b, w_in, w_out, n_tp):
    tok, width = a.shape[2:]
    ffl = w_out.shape[0]
    rows = 2 * tok
    outs = [
        jax.ShapeDtypeStruct((2 * ffl, rows), BF16),
        jax.ShapeDtypeStruct((ffl, rows), BF16),
    ]
    if part:
        outs.append(jax.ShapeDtypeStruct((2, n_tp, tok, width), BF16))
    flops = 2 * rows * ffl * n_tp * width * (5 if part else 3)
    vmem = pl.BlockSpec(memory_space=pltpu.VMEM)
    hbm = pl.BlockSpec(memory_space=pl.ANY)
    return pl.pallas_call(
        functools.partial(rows_kernel, n_tp, part),
        out_shape=outs,
        in_specs=[pl.BlockSpec(memory_space=pltpu.SMEM), vmem, hbm, hbm, hbm, hbm],
        out_specs=[vmem] * len(outs),
        scratch_shapes=[
            pltpu.VMEM((n_tp, rows, width), BF16),
            pltpu.VMEM((n_tp, rows, width), BF16),
            pltpu.VMEM((n_tp, 2 * ffl, width), BF16),
            pltpu.VMEM((n_tp, ffl, width), BF16),
            pltpu.VMEM((3 * ffl, rows), F32),
            pltpu.SemaphoreType.DMA((n_tp, 6)),
        ],
        compiler_params=pltpu.CompilerParams(vmem_limit_bytes=VMEM_LIMIT),
        cost_estimate=pl.CostEstimate(
            flops=flops,
            bytes_accessed=2 * (3 * ffl + 2 * rows) * n_tp * width,
            transcendentals=rows * ffl,
        ),
        name="rows",
    )(t, p, a, b, w_in, w_out)


def grads_kernel(n_tp, chunks, t_ref, *refs):
    dadb_refs, hid_refs = refs[:chunks], refs[chunks : 2 * chunks]
    a_refs, b_refs = refs[2 * chunks : 3 * chunks], refs[3 * chunks : 4 * chunks]
    gin_ref, gout_ref, lhs, xs, gs, oi, oo, sems, osems = refs[4 * chunks :]
    width = xs.shape[2]
    pairs = n_tp // 2
    tok = xs.shape[1] // (2 * chunks)
    ffl = oo.shape[1]

    def fetch(d):
        copies = []
        for c in range(chunks):
            src = (a_refs, b_refs)[d % 2][c]
            for j in range(2):
                for k, dst in enumerate((xs, gs)):
                    copies.append(
                        pltpu.make_async_copy(
                            src.at[j * pairs + d // 2, k],
                            dst.at[d % 2, pl.ds((2 * c + j) * tok, tok)],
                            sems.at[d % 2, 2 * c + j, k],
                        )
                    )
        for copy in copies:
            copy.start()
        return copies

    coming = fetch(0)
    for c in range(chunks):
        lhs[pl.ds(0, 2 * ffl), pl.ds(2 * c * tok, 2 * tok)] = dadb_refs[c][...]
        lhs[pl.ds(2 * ffl, ffl), pl.ds(2 * c * tok, 2 * tok)] = hid_refs[c][...]
    leaving = {}
    tile = min(256, width)
    for d in range(n_tp):
        slot = d % 2
        for copy in coming:
            copy.wait()
        if d + 1 < n_tp:
            coming = fetch(d + 1)
        for copy in leaving.pop(d - 2, ()):
            copy.wait()

        def step(i, _, slot=slot):
            cols = pl.ds(pl.multiple_of(i * tile, tile), tile)
            gi = jnp.dot(lhs[pl.ds(0, 2 * ffl)], xs[slot, :, cols], preferred_element_type=F32)
            oi[slot, :, cols] = gi.astype(BF16)
            go = jnp.dot(lhs[pl.ds(2 * ffl, ffl)], gs[slot, :, cols], preferred_element_type=F32)
            oo[slot, :, cols] = (2.0 * go).astype(BF16)
            return 0

        lax.fori_loop(0, width // tile, step, 0)
        column = pl.ds(pl.multiple_of((t_ref[0] ^ d) * width, width), width)
        leaving[d] = (
            pltpu.make_async_copy(oi.at[slot], gin_ref.at[:, column], osems.at[slot, 0]),
            pltpu.make_async_copy(oo.at[slot], gout_ref.at[:, column], osems.at[slot, 1]),
        )
        for copy in leaving[d]:
            copy.start()
    for copies in leaving.values():
        for copy in copies:
            copy.wait()


def grads_call(t, dadb, hid, a, b, n_tp):
    chunks = len(dadb)
    tok, width = a[0].shape[2:]
    ffl = hid[0].shape[0]
    rows = 2 * tok * chunks
    depth = n_tp * width
    vmem = pl.BlockSpec(memory_space=pltpu.VMEM)
    hbm = pl.BlockSpec(memory_space=pl.ANY)
    return pl.pallas_call(
        functools.partial(grads_kernel, n_tp, chunks),
        out_shape=[
            jax.ShapeDtypeStruct((2 * ffl, depth), BF16),
            jax.ShapeDtypeStruct((ffl, depth), BF16),
        ],
        in_specs=[pl.BlockSpec(memory_space=pltpu.SMEM)]
        + [vmem] * (2 * chunks)
        + [hbm] * (2 * chunks),
        out_specs=[hbm, hbm],
        scratch_shapes=[
            pltpu.VMEM((3 * ffl, rows), BF16),
            pltpu.VMEM((2, rows, width), BF16),
            pltpu.VMEM((2, rows, width), BF16),
            pltpu.VMEM((2, 2 * ffl, width), BF16),
            pltpu.VMEM((2, ffl, width), BF16),
            pltpu.SemaphoreType.DMA((2, 2 * chunks, 2)),
            pltpu.SemaphoreType.DMA((2, 2)),
        ],
        compiler_params=pltpu.CompilerParams(vmem_limit_bytes=VMEM_LIMIT),
        cost_estimate=pl.CostEstimate(
            flops=6 * rows * ffl * depth,
            bytes_accessed=2 * (3 * ffl + 2 * rows) * depth,
            transcendentals=0,
        ),
        name="grads",
    )(t, *dadb, *hid, *a, *b)


def scales(routes, probs, n_ep):
    experts = n_ep // 2
    hit = (routes % experts)[None] == jnp.arange(experts, dtype=jnp.int32)[:, None, None]
    own = jnp.sum(jnp.where(hit, probs.astype(F32)[None], 0.0), axis=2)
    every = lax.all_gather(own, "ep", axis=0)
    me = lax.axis_index("ep")
    order = jnp.arange(n_ep, dtype=jnp.int32)
    block = (order[:, None] ^ me) == order[None, :]
    expert = jnp.arange(experts, dtype=jnp.int32) == me % experts
    pick = block[:, :, None, None] & expert[None, None, :, None]
    return jnp.sum(jnp.where(pick, every[None], 0.0), axis=(1, 2))


def body(tokens, out_grad, routes, probs, w_in, w_out):
    n_ep, n_tp = lax.axis_size("ep"), lax.axis_size("tp")
    pairs = n_tp // 2
    chunks = n_ep // 2
    ffl = w_out.shape[1]
    w_in = w_in.reshape(2 * ffl, w_in.shape[3])
    w_out = w_out[0]
    t = lax.axis_index("tp").astype(jnp.int32).reshape(1)
    p = scales(routes, probs, n_ep)

    lanes = Lanes(2)
    have = {frozenset(): {2: jnp.stack([tokens, out_grad])}}

    def held(name, part):
        parts = have[name]
        if part in parts:
            return parts[part]
        if part < 2:
            return parts[2][part]
        parts[2] = jnp.stack([parts[0], parts[1]])
        return parts[2]

    chunk_of = {}
    for c in range(chunks):
        names = [name_of(2 * c + j, y) for j in range(2) for y in range(pairs)]
        chunk_of.update({name: (c, names) for name in names})
    missing = {c: 2 * pairs * 2 for c in range(chunks)}
    missing[0] -= 2
    a, b = {}, {}
    for target, bit, part in gather_plan(n_ep, n_tp):
        target = frozenset(target)
        source = target - {bit}
        have.setdefault(target, {})[part] = lanes.send(held(source, part), bit)
        c, names = chunk_of[target]
        missing[c] -= 2 if part == 2 else 1
        if not missing[c]:
            a[c] = jnp.stack([held(name, 2) for name in names])
            b[c] = lanes.send(a[c], "t0")

    dadb, hid, parts = {}, {}, {}
    for c in range(chunks):
        near = c < chunks // 2
        scale = p[2 * c : 2 * c + 2].reshape(1, -1)
        out = rows_call(near, t, scale, a[c], b[c], w_in, w_out, n_tp)
        dadb[c], hid[c] = out[:2]
        if near:
            parts[c] = out[2]

    terms = {}
    for c in range(chunks // 2):
        far = lanes.send(parts[c][1], "t0")
        both = (parts[c][0].astype(F32) + far.astype(F32)).astype(BF16)
        for j in range(2):
            for y in range(pairs):
                terms[name_of(2 * c + j, y)] = both[j * pairs + y]
    for target, bit, part in reversed(gather_plan(n_ep, n_tp)):
        target = frozenset(target)
        if target not in terms:
            continue
        half = terms[target].shape[0] // 2
        rows = slice(0, None) if part == 2 else slice(part * half, (part + 1) * half)
        come = lanes.send(terms[target][rows], bit)
        into = terms[target - {bit}]
        if part == 2:
            total = (into.astype(F32) + come.astype(F32)).astype(BF16)
        else:
            total = (into[rows].astype(F32) + come.astype(F32)).astype(BF16)
            halves = [into[:half], into[half:]]
            halves[part] = total
            total = jnp.concatenate(halves)
        terms[target - {bit}] = total
    in_grad = terms[frozenset()]

    order = range(chunks)
    grad_in, grad_out = grads_call(
        t, [dadb[c] for c in order], [hid[c] for c in order],
        [a[c] for c in order], [b[c] for c in order], n_tp,
    )
    return in_grad, grad_in.reshape(1, 2, ffl, -1), grad_out[None]


def solution(mesh):
    return jax.shard_map(
        body,
        mesh=mesh,
        in_specs=(
            P("ep", "tp"),
            P("ep", "tp"),
            P("ep", None),
            P("ep", None),
            P("ep", None, "tp", None),
            P("ep", "tp", None),
        ),
        out_specs=(P("ep", "tp"), P("ep", None, "tp", None), P("ep", "tp", None)),
        check_vma=False,
    )
```

```python
import functools

import jax
import jax.numpy as jnp
from jax import lax
from jax.experimental import pallas as pl
from jax.experimental.pallas import tpu as pltpu
from jax.sharding import PartitionSpec as P

BF16 = jnp.bfloat16
F32 = jnp.float32
VMEM_LIMIT = 58 * 1024 * 1024
SLOTS = 3
SHRINK = 1.0 / 64.0


def hop(block, axis, bit):
    count = lax.axis_size(axis)
    return lax.ppermute(block, axis, [(i, i ^ bit) for i in range(count)])


def leap(block, ep, tp):
    wide, count = lax.axis_size("tp"), lax.axis_size("ep") * lax.axis_size("tp")
    apart = ep * wide + tp
    return lax.ppermute(block, ("ep", "tp"), [(i, i ^ apart) for i in range(count)])


def after(value, *others):
    return lax.optimization_barrier((value,) + others)[0] if others else value


def bits_of(number, letter, skip=0):
    return [f"{letter}{i}" for i in range(skip, number.bit_length() - 1)]


class Lanes:
    def __init__(self, depth):
        self.depth = depth
        self.sent = {}

    def send(self, block, bit, *others):
        queue = self.sent.setdefault(bit, [])
        ready = list(others)
        if bit != "t0":
            ready += queue[-self.depth : len(queue) - self.depth + 1]
        axis = "ep" if bit[0] == "e" else "tp"
        queue.append(hop(after(block, *ready), axis, 1 << int(bit[1:])))
        return queue[-1]


def gather_plan(n_ep, n_tp):
    if (n_ep, n_tp) == (8, 4):
        x, n, f, y = "e0", "e1", "e2", "t1"
        near = (x, n), (y, n), (x, y, n)
        far = (x, f), (y, f), (n, f)
        return [
            ((x,), x, 2), ((y,), y, 2), ((n,), n, 2), ((f,), f, 2),
            ((x, y), x, 0), ((x, y), y, 1),
            ((x, n), x, 2, (f,)), ((y, n), y, 2, (f,)), ((x, y, n), n, 2, (f,)),
            ((x, f), x, 2, *near), ((y, f), y, 2, *near), ((n, f), n, 2, *near),
            ((x, y, f), x, 2, *far, 0), ((y, n, f), y, 2, *far, 0), ((x, n, f), n, 2, *far, 0),
            ((x, y, n, f), x, 0, 1), ((x, y, n, f), y, 1, 1),
        ]
    bits = bits_of(n_ep, "e") + bits_of(n_tp, "t", 1)
    plan = []
    for i, bit in enumerate(bits):
        for low in range(1 << i):
            below = tuple(b for j, b in enumerate(bits[:i]) if low >> j & 1)
            plan.append((below + (bit,), bit, 2))
    return plan


def name_of(ep, tp):
    names = [f"e{i}" for i in range(ep.bit_length()) if ep >> i & 1]
    names += [f"t{i + 1}" for i in range(tp.bit_length()) if tp >> i & 1]
    return frozenset(names)


def rows_of(refs, tok):
    if len(refs) == 1:
        return refs[0].at[0:tok], refs[0].at[tok : 2 * tok], refs[0].at[2 * tok : 2 * tok + 16]
    return refs[0], refs[1].at[0:tok], refs[1].at[tok : tok + 16]


def weights_row(ref, expert, tok):
    width = ref.shape[1]
    per = width // tok
    table = ref[...].astype(F32)
    lines = lax.broadcasted_iota(jnp.int32, table.shape, 0)
    lanes = lax.broadcasted_iota(jnp.int32, table.shape, 1)
    table = jnp.where((lines == expert // per) & (lanes // tok == expert % per), table, 0.0)
    line = jnp.sum(table, axis=0, keepdims=True)
    return functools.reduce(jnp.add, [line[:, i * tok : (i + 1) * tok] for i in range(per)])


def rows_kernel(n_tp, sizes, part, where_ref, win_ref, wout_ref, *refs):
    blocks = len(sizes) // n_tp
    pieces = [[] for _ in range(blocks)]
    for k, size in enumerate(sizes):
        pieces[k // n_tp].append(refs[:size])
        refs = refs[size:]
    if part:
        dadb_ref, hid_ref, part_ref, *refs = refs
    else:
        dadb_ref, hid_ref, *refs = refs
    xs, gs, ps, wi, wo, acc, sems, psems, wsems = refs
    ffl = hid_ref.shape[0]
    tok = hid_ref.shape[1] // blocks
    width = wout_ref.shape[1] // n_tp

    def column(d):
        return pl.ds(pl.multiple_of((where_ref[0] ^ d) * width, width), width)

    copies = []
    for d in range(n_tp):
        mine = []
        for j in range(blocks):
            x, g, _ = rows_of(pieces[j][d], tok)
            into = pl.ds(j * tok, tok)
            mine.append(pltpu.make_async_copy(x, xs.at[d, into], sems.at[d, j, 0]))
            mine.append(pltpu.make_async_copy(g, gs.at[d, into], sems.at[d, j, 1]))
        mine.append(pltpu.make_async_copy(win_ref.at[:, column(d)], wi.at[d], wsems.at[d, 0]))
        mine.append(pltpu.make_async_copy(wout_ref.at[:, column(d)], wo.at[d], wsems.at[d, 1]))
        copies.append(mine)
    tables = []
    for j in range(blocks):
        table = rows_of(pieces[j][0], tok)[2]
        tables.append(pltpu.make_async_copy(table, ps.at[j], psems.at[j]))
        tables[j].start()

    for copy in copies[0] + copies[1]:
        copy.start()
    last = (((1,), (1,)), ((), ()))
    for d in range(n_tp):
        for copy in copies[d]:
            copy.wait()
        for copy in copies[d + 2] if d + 2 < n_tp else ():
            copy.start()
        x = xs[d]
        g = gs[d] * jnp.asarray(SHRINK, BF16)
        ab = lax.dot_general(wi[d], x, last, preferred_element_type=F32)
        h = lax.dot_general(wo[d], g, last, preferred_element_type=F32)
        if d == 0:
            acc[pl.ds(0, 2 * ffl)] = ab
            acc[pl.ds(2 * ffl, ffl)] = h
        else:
            acc[pl.ds(0, 2 * ffl)] += ab
            acc[pl.ds(2 * ffl, ffl)] += h
    scale = []
    for j in range(blocks):
        tables[j].wait()
        first = weights_row(ps.at[j], where_ref[1], tok)
        scale.append(first + weights_row(ps.at[j], where_ref[2], tok))
    scale = jnp.concatenate(scale, axis=1)
    a = acc[pl.ds(0, ffl)]
    b = acc[pl.ds(ffl, ffl)]
    named = scale > 0.0
    dh = acc[pl.ds(2 * ffl, ffl)] * (scale * (1.0 / SHRINK))
    sig = jax.nn.sigmoid(a)
    silu = a * sig
    da = dh * b * sig * (1.0 + a * (1.0 - sig))
    dadb_ref[pl.ds(0, ffl)] = jnp.where(named, da, 0.0).astype(BF16)
    dadb_ref[pl.ds(ffl, ffl)] = jnp.where(named, dh * silu, 0.0).astype(BF16)
    hid_ref[...] = jnp.where(named, (0.5 * scale) * (silu * b), 0.0).astype(BF16)
    if part:
        lhs = dadb_ref[...].T
        for d in range(n_tp):
            out = jnp.dot(lhs, wi[d], preferred_element_type=F32).astype(BF16)
            for j in range(blocks):
                part_ref[d % 2, j * (n_tp // 2) + d // 2] = out[j * tok : (j + 1) * tok]


def rows_call(part, where, pieces, w_in, w_out, tok):
    n_tp = len(pieces[0])
    flat = [piece for block in pieces for piece in block]
    sizes = [len(piece) for piece in flat]
    arrays = [array for piece in flat for array in piece]
    blocks = len(pieces)
    rows, width = blocks * tok, arrays[0].shape[1]
    ffl = w_out.shape[0]
    outs = [
        jax.ShapeDtypeStruct((2 * ffl, rows), BF16),
        jax.ShapeDtypeStruct((ffl, rows), BF16),
    ]
    if part:
        outs.append(jax.ShapeDtypeStruct((2, blocks * n_tp // 2, tok, width), BF16))
    vmem = pl.BlockSpec(memory_space=pltpu.VMEM)
    hbm = pl.BlockSpec(memory_space=pltpu.HBM)
    return pl.pallas_call(
        functools.partial(rows_kernel, n_tp, sizes, part),
        out_shape=outs,
        in_specs=[pl.BlockSpec(memory_space=pltpu.SMEM)] + [hbm] * (2 + len(arrays)),
        out_specs=[vmem] * len(outs),
        scratch_shapes=[
            pltpu.VMEM((n_tp, rows, width), BF16),
            pltpu.VMEM((n_tp, rows, width), BF16),
            pltpu.VMEM((blocks, 16, width), BF16),
            pltpu.VMEM((n_tp, 2 * ffl, width), BF16),
            pltpu.VMEM((n_tp, ffl, width), BF16),
            pltpu.VMEM((3 * ffl, rows), F32),
            pltpu.SemaphoreType.DMA((n_tp, blocks, 2)),
            pltpu.SemaphoreType.DMA((blocks,)),
            pltpu.SemaphoreType.DMA((n_tp, 2)),
        ],
        compiler_params=pltpu.CompilerParams(vmem_limit_bytes=VMEM_LIMIT),
        cost_estimate=pl.CostEstimate(
            flops=2 * rows * ffl * n_tp * width * (5 if part else 3),
            bytes_accessed=2 * (3 * ffl + 2 * rows) * n_tp * width,
            transcendentals=rows * ffl,
        ),
        name="rows",
    )(where, w_in, w_out, *arrays)


def grads_kernel(steps, sizes, added, filled, where_ref, dadb_ref, hid_ref, *refs):
    pieces = []
    tok = hid_ref.shape[1] * len(steps) // len(sizes)
    for size in sizes:
        pieces.append(rows_of(refs[:size], tok))
        refs = refs[size:]
    base, refs = (refs[:2], refs[2:]) if added else ((), refs)
    gin_ref, gout_ref, xs, gs, oi, oo, bi, bo, sems, bsems, osems = refs[2 if filled else 0 :]
    width = pieces[0][0].shape[1]
    slots, _, tile = xs.shape
    tiles = width // tile
    total = len(steps) * tiles

    def column(k):
        start = (where_ref[0] ^ steps[k // tiles]) * width + k % tiles * tile
        return pl.ds(pl.multiple_of(start, tile), tile)

    def fetch(k):
        slot, cols = k % slots, pl.ds(k % tiles * tile, tile)
        copies = []
        for i, (x, g, _) in enumerate(pieces[k // tiles :: len(steps)]):
            into = pl.ds(i * tok, tok)
            copies.append(pltpu.make_async_copy(x.at[:, cols], xs.at[slot, into], sems.at[slot, i, 0]))
            copies.append(pltpu.make_async_copy(g.at[:, cols], gs.at[slot, into], sems.at[slot, i, 1]))
        for i, (src, dst) in enumerate(zip(base, (bi, bo))):
            copies.append(pltpu.make_async_copy(src.at[:, column(k)], dst.at[slot], bsems.at[slot, i]))
        for copy in copies:
            copy.start()
        return copies

    coming = [fetch(k) for k in range(min(slots - 1, total))]
    leaving = {}
    for k in range(total):
        slot = k % slots
        if k + slots - 1 < total:
            coming.append(fetch(k + slots - 1))
        for copy in coming[k]:
            copy.wait()
        for copy in leaving.pop(k - slots, ()):
            copy.wait()
        gi = jnp.dot(dadb_ref[...], xs[slot], preferred_element_type=F32)
        go = 2.0 * jnp.dot(hid_ref[...], gs[slot], preferred_element_type=F32)
        if added:
            gi = gi + bi[slot].astype(F32)
            go = go + bo[slot].astype(F32)
        oi[slot] = gi.astype(BF16)
        oo[slot] = go.astype(BF16)
        leaving[k] = (
            pltpu.make_async_copy(oi.at[slot], gin_ref.at[:, column(k)], osems.at[slot, 0]),
            pltpu.make_async_copy(oo.at[slot], gout_ref.at[:, column(k)], osems.at[slot, 1]),
        )
        for copy in leaving[k]:
            copy.start()
    for copies in leaving.values():
        for copy in copies:
            copy.wait()


def grads_call(where, dadb, hid, pieces, steps, base=(), filled=()):
    n_tp = len(pieces[0])
    flat = [block[d] for block in pieces for d in steps]
    sizes = [len(piece) for piece in flat]
    arrays = [array for piece in flat for array in piece]
    width = arrays[0].shape[1]
    ffl, rows = hid.shape
    depth = n_tp * width
    tile = min(512, width)
    vmem = pl.BlockSpec(memory_space=pltpu.VMEM)
    hbm = pl.BlockSpec(memory_space=pltpu.HBM)
    operands = [where, dadb, hid, *arrays, *base, *filled]
    return pl.pallas_call(
        functools.partial(grads_kernel, steps, sizes, len(base) > 0, len(filled) > 0),
        out_shape=[
            jax.ShapeDtypeStruct((2 * ffl, depth), BF16),
            jax.ShapeDtypeStruct((ffl, depth), BF16),
        ],
        in_specs=[pl.BlockSpec(memory_space=pltpu.SMEM), vmem, vmem]
        + [hbm] * (len(operands) - 3),
        out_specs=[hbm, hbm],
        input_output_aliases={len(operands) - 2: 0, len(operands) - 1: 1} if filled else {},
        scratch_shapes=[
            pltpu.VMEM((SLOTS, rows, tile), BF16),
            pltpu.VMEM((SLOTS, rows, tile), BF16),
            pltpu.VMEM((SLOTS, 2 * ffl, tile), BF16),
            pltpu.VMEM((SLOTS, ffl, tile), BF16),
            pltpu.VMEM((SLOTS, 2 * ffl, tile), BF16),
            pltpu.VMEM((SLOTS, ffl, tile), BF16),
            pltpu.SemaphoreType.DMA((SLOTS, len(pieces), 2)),
            pltpu.SemaphoreType.DMA((SLOTS, 2)),
            pltpu.SemaphoreType.DMA((SLOTS, 2)),
        ],
        compiler_params=pltpu.CompilerParams(vmem_limit_bytes=VMEM_LIMIT),
        cost_estimate=pl.CostEstimate(
            flops=6 * rows * ffl * len(steps) * width,
            bytes_accessed=2 * (3 * ffl + 2 * rows) * len(steps) * width,
            transcendentals=0,
        ),
        name="grads",
    )(*operands)


def own_rows(tokens, out_grad, routes, probs, n_ep):
    tok, width = tokens.shape
    copies = jnp.arange(n_ep, dtype=jnp.int32)[:, None, None]
    table = jnp.sum(jnp.where(routes[None] == copies, probs[None], 0), axis=2).astype(BF16)
    table = table.reshape(n_ep * tok // width, width)
    table = jnp.pad(table, ((0, 16 - table.shape[0]), (0, 0)))
    return jnp.concatenate([tokens, out_grad, table])


def body(tokens, out_grad, routes, probs, w_in, w_out):
    n_ep, n_tp = lax.axis_size("ep"), lax.axis_size("tp")
    pairs = n_tp // 2
    ffl = w_out.shape[1]
    w_in = w_in.reshape(2 * ffl, w_in.shape[3])
    w_out = w_out[0]
    tok = tokens.shape[0]
    expert = lax.axis_index("ep") % (n_ep // 2)
    where = jnp.stack([lax.axis_index("tp"), expert, expert + n_ep // 2]).astype(jnp.int32)

    lanes = Lanes(1)
    have = {frozenset(): {2: own_rows(tokens, out_grad, routes, probs, n_ep)}}

    def held(name, part):
        parts = have[name]
        if part not in parts:
            if part == 2:
                parts[2] = jnp.concatenate([parts[0], parts[1]])
            else:
                parts[part] = parts[2][:tok] if part == 0 else parts[2][tok:]
        return parts[part]

    def arrays(name):
        parts = have[name]
        return (parts[2],) if 2 in parts else (parts[0], parts[1])

    names = [[name_of(e, y) for y in range(pairs)] for e in range(n_ep)]
    half_of = {name: 2 * e // n_ep for e in range(n_ep) for name in names[e]}
    missing = [n_ep * pairs - 2, n_ep * pairs]
    pieces = [None] * n_ep
    done = []
    terms = {}
    other = {frozenset(): (lanes.send(have[frozenset()][2], "t0"),)}
    for target, bit, part, *first in gather_plan(n_ep, n_tp):
        target = frozenset(target)
        before = []
        for what in first:
            before.append(done[what] if isinstance(what, int) else have[frozenset(what)][2])
        have.setdefault(target, {})[part] = lanes.send(held(target - {bit}, part), bit, *before)
        if 2 in have[target] or len(have[target]) == 2:
            other[target] = tuple(lanes.send(array, "t0") for array in arrays(target))
        half = half_of[target]
        missing[half] -= 2 if part == 2 else 1
        if missing[half]:
            continue
        blocks = range(half * n_ep // 2, (half + 1) * n_ep // 2)
        for e in blocks:
            pieces[e] = [
                arrays(names[e][d // 2]) if d % 2 == 0 else other[names[e][d // 2]]
                for d in range(n_tp)
            ]
        mine = pieces[blocks[0] : blocks[-1] + 1]
        out = rows_call(half == 0, where, mine, w_in, w_out, tok)
        if half == 0:
            count = len(blocks) * pairs
            step = max(1, count // 2)
            for i in range(0, count, step):
                come = lanes.send(out[2][1, i : i + step], "t0")
                total = (out[2][0, i : i + step].astype(F32) + come.astype(F32)).astype(BF16)
                for k in range(step):
                    terms[names[(i + k) // pairs][(i + k) % pairs]] = total[k]
            near = grads_call(where, out[0], out[1], mine, list(range(n_tp)))
            done += [out[1], hop(near[1][:16, :128], "tp", 1)]
        else:
            last = out[1]
            grads = grads_call(where, out[0], out[1], mine, list(range(n_tp)), near)

    keep = {}
    for e in range(n_ep // 2):
        for y in range(pairs):
            keep[e, y] = terms[names[e][y]].astype(F32)
    top = n_ep // 4
    for e in range(n_ep // 2 - 1, top, -1):
        for y in range(pairs):
            if y and e > top:
                keep[e - top, y] += hop(keep[e, y].astype(BF16), "ep", top).astype(F32)
            elif e > top:
                keep[top, 0] += hop(keep[e, y].astype(BF16), "ep", e - top).astype(F32)
    for y in range(1, pairs):
        keep[top, 0] += hop(keep[top, y].astype(BF16), "tp", 2 * y).astype(F32)
    total = keep[0, 0]
    for e in range(top + 1):
        for y in range(pairs if e < top else 1):
            if e or y:
                sums = keep[e, y].astype(BF16)
                total = total + leap(after(sums, last) if True else sums, e, 2 * y).astype(F32)
    in_grad = total.astype(BF16)

    grad_in, grad_out = grads
    return in_grad, grad_in.reshape(1, 2, ffl, -1), grad_out[None]


def solution(mesh):
    return jax.shard_map(
        body,
        mesh=mesh,
        in_specs=(
            P("ep", "tp"),
            P("ep", "tp"),
            P("ep", None),
            P("ep", None),
            P("ep", None, "tp", None),
            P("ep", "tp", None),
        ),
        out_specs=(P("ep", "tp"), P("ep", None, "tp", None), P("ep", "tp", None)),
        check_vma=False,
    )
```

```python
import functools

import jax
import jax.numpy as jnp
from jax import lax
from jax.experimental import pallas as pl
from jax.experimental.pallas import tpu as pltpu
from jax.sharding import PartitionSpec as P

BF16 = jnp.bfloat16
F32 = jnp.float32
VMEM_LIMIT = 58 * 1024 * 1024
SLOTS = 3
SHRINK = 1.0 / 64.0


def hop(block, axis, bit):
    count = lax.axis_size(axis)
    return lax.ppermute(block, axis, [(i, i ^ bit) for i in range(count)])


def leap(block, ep, tp):
    wide, count = lax.axis_size("tp"), lax.axis_size("ep") * lax.axis_size("tp")
    apart = ep * wide + tp
    return lax.ppermute(block, ("ep", "tp"), [(i, i ^ apart) for i in range(count)])


def after(value, *others):
    return lax.optimization_barrier((value,) + others)[0] if others else value


def bits_of(number, letter, skip=0):
    return [f"{letter}{i}" for i in range(skip, number.bit_length() - 1)]


class Lanes:
    def __init__(self, depth):
        self.depth = depth
        self.sent = {}

    def send(self, block, bit, *others):
        queue = self.sent.setdefault(bit, [])
        ready = list(others)
        if bit != "t0":
            ready += queue[-self.depth : len(queue) - self.depth + 1]
        axis = "ep" if bit[0] == "e" else "tp"
        queue.append(hop(after(block, *ready), axis, 1 << int(bit[1:])))
        return queue[-1]


def gather_plan(n_ep, n_tp):
    if (n_ep, n_tp) == (8, 4):
        x, n, f, y = "e0", "e1", "e2", "t1"
        near = (x, n), (y, n), (x, y, n)
        far = (x, f), (y, f), (n, f)
        return [
            ((x,), x, 2), ((y,), y, 2), ((n,), n, 2), ((f,), f, 2),
            ((x, y), x, 0), ((x, y), y, 1),
            ((x, n), x, 2, (f,)), ((y, n), y, 2, (f,)), ((x, y, n), n, 2, (f,)),
            ((x, f), x, 2, *near), ((y, f), y, 2, *near), ((n, f), n, 2, *near),
            ((x, y, f), x, 2, *far, 0), ((y, n, f), y, 2, *far, 0), ((x, n, f), n, 2, *far, 0),
            ((x, y, n, f), x, 0), ((x, y, n, f), y, 1),
        ]
    bits = bits_of(n_ep, "e") + bits_of(n_tp, "t", 1)
    plan = []
    for i, bit in enumerate(bits):
        for low in range(1 << i):
            below = tuple(b for j, b in enumerate(bits[:i]) if low >> j & 1)
            plan.append((below + (bit,), bit, 2))
    return plan


def name_of(ep, tp):
    names = [f"e{i}" for i in range(ep.bit_length()) if ep >> i & 1]
    names += [f"t{i + 1}" for i in range(tp.bit_length()) if tp >> i & 1]
    return frozenset(names)


def rows_of(refs, tok):
    if len(refs) == 1:
        return refs[0].at[0:tok], refs[0].at[tok : 2 * tok], refs[0].at[2 * tok : 2 * tok + 16]
    return refs[0], refs[1].at[0:tok], refs[1].at[tok : tok + 16]


def weights_row(ref, expert, tok):
    width = ref.shape[1]
    per = width // tok
    table = ref[...].astype(F32)
    lines = lax.broadcasted_iota(jnp.int32, table.shape, 0)
    lanes = lax.broadcasted_iota(jnp.int32, table.shape, 1)
    table = jnp.where((lines == expert // per) & (lanes // tok == expert % per), table, 0.0)
    line = jnp.sum(table, axis=0, keepdims=True)
    return functools.reduce(jnp.add, [line[:, i * tok : (i + 1) * tok] for i in range(per)])


def rows_kernel(n_tp, sizes, part, where_ref, win_ref, wout_ref, *refs):
    blocks = len(sizes) // n_tp
    pieces = [[] for _ in range(blocks)]
    for k, size in enumerate(sizes):
        pieces[k // n_tp].append(refs[:size])
        refs = refs[size:]
    if part:
        dadb_ref, hid_ref, *part_refs = refs[:5]
        refs = refs[5:]
    else:
        dadb_ref, hid_ref, *refs = refs
    xs, gs, ps, wi, wo, acc, sems, psems, wsems = refs
    ffl = hid_ref.shape[0]
    tok = hid_ref.shape[1] // blocks
    width = wout_ref.shape[1] // n_tp

    def column(d):
        return pl.ds(pl.multiple_of((where_ref[0] ^ d) * width, width), width)

    copies = []
    for d in range(n_tp):
        mine = []
        for j in range(blocks):
            x, g, _ = rows_of(pieces[j][d], tok)
            into = pl.ds(j * tok, tok)
            mine.append(pltpu.make_async_copy(x, xs.at[d, into], sems.at[d, j, 0]))
            mine.append(pltpu.make_async_copy(g, gs.at[d, into], sems.at[d, j, 1]))
        mine.append(pltpu.make_async_copy(win_ref.at[:, column(d)], wi.at[d], wsems.at[d, 0]))
        mine.append(pltpu.make_async_copy(wout_ref.at[:, column(d)], wo.at[d], wsems.at[d, 1]))
        copies.append(mine)
    tables = []
    for j in range(blocks):
        table = rows_of(pieces[j][0], tok)[2]
        tables.append(pltpu.make_async_copy(table, ps.at[j], psems.at[j]))
        tables[j].start()

    for copy in copies[0] + copies[1]:
        copy.start()
    last = (((1,), (1,)), ((), ()))
    for d in range(n_tp):
        for copy in copies[d]:
            copy.wait()
        for copy in copies[d + 2] if d + 2 < n_tp else ():
            copy.start()
        x = xs[d]
        g = gs[d] * jnp.asarray(SHRINK, BF16)
        ab = lax.dot_general(wi[d], x, last, preferred_element_type=F32)
        h = lax.dot_general(wo[d], g, last, preferred_element_type=F32)
        if d == 0:
            acc[pl.ds(0, 2 * ffl)] = ab
            acc[pl.ds(2 * ffl, ffl)] = h
        else:
            acc[pl.ds(0, 2 * ffl)] += ab
            acc[pl.ds(2 * ffl, ffl)] += h
    scale = []
    for j in range(blocks):
        tables[j].wait()
        first = weights_row(ps.at[j], where_ref[1], tok)
        scale.append(first + weights_row(ps.at[j], where_ref[2], tok))
    scale = jnp.concatenate(scale, axis=1)
    a = acc[pl.ds(0, ffl)]
    b = acc[pl.ds(ffl, ffl)]
    named = scale > 0.0
    dh = acc[pl.ds(2 * ffl, ffl)] * (scale * (1.0 / SHRINK))
    sig = jax.nn.sigmoid(a)
    silu = a * sig
    da = dh * b * sig * (1.0 + a * (1.0 - sig))
    dadb_ref[pl.ds(0, ffl)] = jnp.where(named, da, 0.0).astype(BF16)
    dadb_ref[pl.ds(ffl, ffl)] = jnp.where(named, dh * silu, 0.0).astype(BF16)
    hid_ref[...] = jnp.where(named, (0.5 * scale) * (silu * b), 0.0).astype(BF16)
    if part:
        lhs = dadb_ref[...].T
        for d in range(n_tp):
            out = jnp.dot(lhs, wi[d], preferred_element_type=F32).astype(BF16)
            for j in range(blocks):
                piece, half = j * (n_tp // 2) + d // 2, blocks * n_tp // 4
                into = part_refs[1 + piece // half] if d % 2 else part_refs[0]
                into[piece % half if d % 2 else piece] = out[j * tok : (j + 1) * tok]


def rows_call(part, where, pieces, w_in, w_out, tok):
    n_tp = len(pieces[0])
    flat = [piece for block in pieces for piece in block]
    sizes = [len(piece) for piece in flat]
    arrays = [array for piece in flat for array in piece]
    blocks = len(pieces)
    rows, width = blocks * tok, arrays[0].shape[1]
    ffl = w_out.shape[0]
    outs = [
        jax.ShapeDtypeStruct((2 * ffl, rows), BF16),
        jax.ShapeDtypeStruct((ffl, rows), BF16),
    ]
    if part:
        outs += [
            jax.ShapeDtypeStruct((blocks * n_tp // k, tok, width), BF16) for k in (2, 4, 4)
        ]
    vmem = pl.BlockSpec(memory_space=pltpu.VMEM)
    hbm = pl.BlockSpec(memory_space=pltpu.HBM)
    return pl.pallas_call(
        functools.partial(rows_kernel, n_tp, sizes, part),
        out_shape=outs,
        in_specs=[pl.BlockSpec(memory_space=pltpu.SMEM)] + [hbm] * (2 + len(arrays)),
        out_specs=[vmem] * len(outs),
        scratch_shapes=[
            pltpu.VMEM((n_tp, rows, width), BF16),
            pltpu.VMEM((n_tp, rows, width), BF16),
            pltpu.VMEM((blocks, 16, width), BF16),
            pltpu.VMEM((n_tp, 2 * ffl, width), BF16),
            pltpu.VMEM((n_tp, ffl, width), BF16),
            pltpu.VMEM((3 * ffl, rows), F32),
            pltpu.SemaphoreType.DMA((n_tp, blocks, 2)),
            pltpu.SemaphoreType.DMA((blocks,)),
            pltpu.SemaphoreType.DMA((n_tp, 2)),
        ],
        compiler_params=pltpu.CompilerParams(vmem_limit_bytes=VMEM_LIMIT),
        cost_estimate=pl.CostEstimate(
            flops=2 * rows * ffl * n_tp * width * (5 if part else 3),
            bytes_accessed=2 * (3 * ffl + 2 * rows) * n_tp * width,
            transcendentals=rows * ffl,
        ),
        name="rows",
    )(where, w_in, w_out, *arrays)


def far_kernel(n_tp, sizes, where_ref, win_ref, wout_ref, *refs):
    blocks = len(sizes) // n_tp
    pieces = [[] for _ in range(blocks)]
    for k, size in enumerate(sizes):
        pieces[k // n_tp].append(refs[:size])
        refs = refs[size:]
    base, refs = refs[:2], refs[2:]
    gin_ref, gout_ref, xs, gs, ps, wi, wo, acc, dadb_ref, hid_ref, bi, bo, oi, oo, *refs = refs
    sems, psems, wsems, bsems, osems = refs
    ffl = hid_ref.shape[0]
    tok = hid_ref.shape[1] // blocks
    width = wout_ref.shape[1] // n_tp

    def column(d):
        return pl.ds(pl.multiple_of((where_ref[0] ^ d) * width, width), width)

    copies = []
    for d in range(n_tp):
        mine = []
        for j in range(blocks):
            x, g, _ = rows_of(pieces[j][d], tok)
            into = pl.ds(j * tok, tok)
            mine.append(pltpu.make_async_copy(x, xs.at[d, into], sems.at[d, j, 0]))
            mine.append(pltpu.make_async_copy(g, gs.at[d, into], sems.at[d, j, 1]))
        mine.append(pltpu.make_async_copy(win_ref.at[:, column(d)], wi.at[d], wsems.at[d, 0]))
        mine.append(pltpu.make_async_copy(wout_ref.at[:, column(d)], wo.at[d], wsems.at[d, 1]))
        copies.append(mine)
    tables = []
    for j in range(blocks):
        table = rows_of(pieces[j][0], tok)[2]
        tables.append(pltpu.make_async_copy(table, ps.at[j], psems.at[j]))
        tables[j].start()

    for copy in copies[0] + copies[1]:
        copy.start()
    last = (((1,), (1,)), ((), ()))
    for d in range(n_tp):
        for copy in copies[d]:
            copy.wait()
        for copy in copies[d + 2] if d + 2 < n_tp else ():
            copy.start()
        if d == n_tp - 2:
            added = [pltpu.make_async_copy(base[0], bi, bsems.at[0])]
            added.append(pltpu.make_async_copy(base[1], bo, bsems.at[1]))
            for copy in added:
                copy.start()
        x = xs[d]
        g = gs[d] * jnp.asarray(SHRINK, BF16)
        ab = lax.dot_general(wi[d], x, last, preferred_element_type=F32)
        h = lax.dot_general(wo[d], g, last, preferred_element_type=F32)
        if d == 0:
            acc[pl.ds(0, 2 * ffl)] = ab
            acc[pl.ds(2 * ffl, ffl)] = h
        else:
            acc[pl.ds(0, 2 * ffl)] += ab
            acc[pl.ds(2 * ffl, ffl)] += h
    scale = []
    for j in range(blocks):
        tables[j].wait()
        first = weights_row(ps.at[j], where_ref[1], tok)
        scale.append(first + weights_row(ps.at[j], where_ref[2], tok))
    scale = jnp.concatenate(scale, axis=1)
    a = acc[pl.ds(0, ffl)]
    b = acc[pl.ds(ffl, ffl)]
    named = scale > 0.0
    dh = acc[pl.ds(2 * ffl, ffl)] * (scale * (1.0 / SHRINK))
    sig = jax.nn.sigmoid(a)
    silu = a * sig
    da = dh * b * sig * (1.0 + a * (1.0 - sig))
    dadb_ref[pl.ds(0, ffl)] = jnp.where(named, da, 0.0).astype(BF16)
    dadb_ref[pl.ds(ffl, ffl)] = jnp.where(named, dh * silu, 0.0).astype(BF16)
    hid_ref[...] = jnp.where(named, (0.5 * scale) * (silu * b), 0.0).astype(BF16)
    for copy in added:
        copy.wait()
    tile = oi.shape[2]
    tiles = width // tile
    leaving = {}
    for k in range(n_tp * tiles):
        slot, d, cols = k % 2, k // tiles, pl.ds(k % tiles * tile, tile)
        start = (where_ref[0] ^ d) * width + k % tiles * tile
        here = pl.ds(pl.multiple_of(start, tile), tile)
        for copy in leaving.pop(k - 2, ()):
            copy.wait()
        gi = jnp.dot(dadb_ref[...], xs[d, :, cols], preferred_element_type=F32)
        go = 2.0 * jnp.dot(hid_ref[...], gs[d, :, cols], preferred_element_type=F32)
        oi[slot] = (gi + bi[:, here].astype(F32)).astype(BF16)
        oo[slot] = (go + bo[:, here].astype(F32)).astype(BF16)
        leaving[k] = (
            pltpu.make_async_copy(oi.at[slot], gin_ref.at[:, here], osems.at[slot, 0]),
            pltpu.make_async_copy(oo.at[slot], gout_ref.at[:, here], osems.at[slot, 1]),
        )
        for copy in leaving[k]:
            copy.start()
    for copies in leaving.values():
        for copy in copies:
            copy.wait()


def far_call(where, pieces, w_in, w_out, tok, base):
    n_tp = len(pieces[0])
    flat = [piece for block in pieces for piece in block]
    sizes = [len(piece) for piece in flat]
    arrays = [array for piece in flat for array in piece]
    blocks = len(pieces)
    rows, width = blocks * tok, arrays[0].shape[1]
    ffl, depth = w_out.shape
    tile = min(512, width)
    hbm = pl.BlockSpec(memory_space=pltpu.HBM)
    return pl.pallas_call(
        functools.partial(far_kernel, n_tp, sizes),
        out_shape=[
            jax.ShapeDtypeStruct((2 * ffl, depth), BF16),
            jax.ShapeDtypeStruct((ffl, depth), BF16),
        ],
        in_specs=[pl.BlockSpec(memory_space=pltpu.SMEM)] + [hbm] * (4 + len(arrays)),
        out_specs=[hbm, hbm],
        scratch_shapes=[
            pltpu.VMEM((n_tp, rows, width), BF16),
            pltpu.VMEM((n_tp, rows, width), BF16),
            pltpu.VMEM((blocks, 16, width), BF16),
            pltpu.VMEM((n_tp, 2 * ffl, width), BF16),
            pltpu.VMEM((n_tp, ffl, width), BF16),
            pltpu.VMEM((3 * ffl, rows), F32),
            pltpu.VMEM((2 * ffl, rows), BF16),
            pltpu.VMEM((ffl, rows), BF16),
            pltpu.VMEM((2 * ffl, depth), BF16),
            pltpu.VMEM((ffl, depth), BF16),
            pltpu.VMEM((2, 2 * ffl, tile), BF16),
            pltpu.VMEM((2, ffl, tile), BF16),
            pltpu.SemaphoreType.DMA((n_tp, blocks, 2)),
            pltpu.SemaphoreType.DMA((blocks,)),
            pltpu.SemaphoreType.DMA((n_tp, 2)),
            pltpu.SemaphoreType.DMA((2,)),
            pltpu.SemaphoreType.DMA((2, 2)),
        ],
        compiler_params=pltpu.CompilerParams(vmem_limit_bytes=VMEM_LIMIT),
        cost_estimate=pl.CostEstimate(
            flops=12 * rows * ffl * depth,
            bytes_accessed=2 * (9 * ffl + 2 * rows) * depth,
            transcendentals=rows * ffl,
        ),
        name="far",
    )(where, w_in, w_out, *arrays, *base)


def grads_kernel(steps, sizes, added, filled, where_ref, dadb_ref, hid_ref, *refs):
    pieces = []
    tok = hid_ref.shape[1] * len(steps) // len(sizes)
    for size in sizes:
        pieces.append(rows_of(refs[:size], tok))
        refs = refs[size:]
    base, refs = (refs[:2], refs[2:]) if added else ((), refs)
    gin_ref, gout_ref, xs, gs, oi, oo, bi, bo, sems, bsems, osems = refs[2 if filled else 0 :]
    width = pieces[0][0].shape[1]
    slots, _, tile = xs.shape
    tiles = width // tile
    total = len(steps) * tiles

    def column(k):
        start = (where_ref[0] ^ steps[k // tiles]) * width + k % tiles * tile
        return pl.ds(pl.multiple_of(start, tile), tile)

    def fetch(k):
        slot, cols = k % slots, pl.ds(k % tiles * tile, tile)
        copies = []
        for i, (x, g, _) in enumerate(pieces[k // tiles :: len(steps)]):
            into = pl.ds(i * tok, tok)
            copies.append(pltpu.make_async_copy(x.at[:, cols], xs.at[slot, into], sems.at[slot, i, 0]))
            copies.append(pltpu.make_async_copy(g.at[:, cols], gs.at[slot, into], sems.at[slot, i, 1]))
        for i, (src, dst) in enumerate(zip(base, (bi, bo))):
            copies.append(pltpu.make_async_copy(src.at[:, column(k)], dst.at[slot], bsems.at[slot, i]))
        for copy in copies:
            copy.start()
        return copies

    coming = [fetch(k) for k in range(min(slots - 1, total))]
    leaving = {}
    for k in range(total):
        slot = k % slots
        if k + slots - 1 < total:
            coming.append(fetch(k + slots - 1))
        for copy in coming[k]:
            copy.wait()
        for copy in leaving.pop(k - slots, ()):
            copy.wait()
        gi = jnp.dot(dadb_ref[...], xs[slot], preferred_element_type=F32)
        go = 2.0 * jnp.dot(hid_ref[...], gs[slot], preferred_element_type=F32)
        if added:
            gi = gi + bi[slot].astype(F32)
            go = go + bo[slot].astype(F32)
        oi[slot] = gi.astype(BF16)
        oo[slot] = go.astype(BF16)
        leaving[k] = (
            pltpu.make_async_copy(oi.at[slot], gin_ref.at[:, column(k)], osems.at[slot, 0]),
            pltpu.make_async_copy(oo.at[slot], gout_ref.at[:, column(k)], osems.at[slot, 1]),
        )
        for copy in leaving[k]:
            copy.start()
    for copies in leaving.values():
        for copy in copies:
            copy.wait()


def grads_call(where, dadb, hid, pieces, steps, base=(), filled=()):
    n_tp = len(pieces[0])
    flat = [block[d] for block in pieces for d in steps]
    sizes = [len(piece) for piece in flat]
    arrays = [array for piece in flat for array in piece]
    width = arrays[0].shape[1]
    ffl, rows = hid.shape
    depth = n_tp * width
    tile = min(512, width)
    vmem = pl.BlockSpec(memory_space=pltpu.VMEM)
    hbm = pl.BlockSpec(memory_space=pltpu.HBM)
    operands = [where, dadb, hid, *arrays, *base, *filled]
    return pl.pallas_call(
        functools.partial(grads_kernel, steps, sizes, len(base) > 0, len(filled) > 0),
        out_shape=[
            jax.ShapeDtypeStruct((2 * ffl, depth), BF16),
            jax.ShapeDtypeStruct((ffl, depth), BF16),
        ],
        in_specs=[pl.BlockSpec(memory_space=pltpu.SMEM), vmem, vmem]
        + [hbm] * (len(operands) - 3),
        out_specs=[hbm, hbm],
        input_output_aliases={len(operands) - 2: 0, len(operands) - 1: 1} if filled else {},
        scratch_shapes=[
            pltpu.VMEM((SLOTS, rows, tile), BF16),
            pltpu.VMEM((SLOTS, rows, tile), BF16),
            pltpu.VMEM((SLOTS, 2 * ffl, tile), BF16),
            pltpu.VMEM((SLOTS, ffl, tile), BF16),
            pltpu.VMEM((SLOTS, 2 * ffl, tile), BF16),
            pltpu.VMEM((SLOTS, ffl, tile), BF16),
            pltpu.SemaphoreType.DMA((SLOTS, len(pieces), 2)),
            pltpu.SemaphoreType.DMA((SLOTS, 2)),
            pltpu.SemaphoreType.DMA((SLOTS, 2)),
        ],
        compiler_params=pltpu.CompilerParams(vmem_limit_bytes=VMEM_LIMIT),
        cost_estimate=pl.CostEstimate(
            flops=6 * rows * ffl * len(steps) * width,
            bytes_accessed=2 * (3 * ffl + 2 * rows) * len(steps) * width,
            transcendentals=0,
        ),
        name="grads",
    )(*operands)


def own_rows(tokens, out_grad, routes, probs, n_ep):
    tok, width = tokens.shape
    copies = jnp.arange(n_ep, dtype=jnp.int32)[:, None, None]
    table = jnp.sum(jnp.where(routes[None] == copies, probs[None], 0), axis=2).astype(BF16)
    table = table.reshape(n_ep * tok // width, width)
    table = jnp.pad(table, ((0, 16 - table.shape[0]), (0, 0)))
    return jnp.concatenate([tokens, out_grad, table])


def body(tokens, out_grad, routes, probs, w_in, w_out):
    n_ep, n_tp = lax.axis_size("ep"), lax.axis_size("tp")
    pairs = n_tp // 2
    ffl = w_out.shape[1]
    w_in = w_in.reshape(2 * ffl, w_in.shape[3])
    w_out = w_out[0]
    tok = tokens.shape[0]
    expert = lax.axis_index("ep") % (n_ep // 2)
    where = jnp.stack([lax.axis_index("tp"), expert, expert + n_ep // 2]).astype(jnp.int32)

    lanes = Lanes(1)
    have = {frozenset(): {2: own_rows(tokens, out_grad, routes, probs, n_ep)}}

    def held(name, part):
        parts = have[name]
        if part not in parts:
            if part == 2:
                parts[2] = jnp.concatenate([parts[0], parts[1]])
            else:
                parts[part] = parts[2][:tok] if part == 0 else parts[2][tok:]
        return parts[part]

    def arrays(name):
        parts = have[name]
        return (parts[2],) if 2 in parts else (parts[0], parts[1])

    names = [[name_of(e, y) for y in range(pairs)] for e in range(n_ep)]
    half_of = {name: 2 * e // n_ep for e in range(n_ep) for name in names[e]}
    missing = [n_ep * pairs - 2, n_ep * pairs]
    pieces = [None] * n_ep
    done = []
    terms = {}
    other = {frozenset(): (lanes.send(have[frozenset()][2], "t0"),)}
    plan = gather_plan(n_ep, n_tp)
    for target, bit, part, *first in plan:
        target = frozenset(target)
        before = []
        for what in first:
            before.append(done[what] if isinstance(what, int) else have[frozenset(what)][2])
        have.setdefault(target, {})[part] = lanes.send(held(target - {bit}, part), bit, *before)
        if 2 in have[target] or len(have[target]) == 2:
            other[target] = tuple(lanes.send(array, "t0") for array in arrays(target))
        half = half_of[target]
        missing[half] -= 2 if part == 2 else 1
        if missing[half]:
            continue
        blocks = range(half * n_ep // 2, (half + 1) * n_ep // 2)
        for e in blocks:
            pieces[e] = [
                arrays(names[e][d // 2]) if d % 2 == 0 else other[names[e][d // 2]]
                for d in range(n_tp)
            ]
        mine = pieces[blocks[0] : blocks[-1] + 1]
        if half == 0:
            out = rows_call(True, where, mine, w_in, w_out, tok)
            near = grads_call(where, out[0], out[1], mine, list(range(n_tp)))
            done += [out[1], hop(near[1][:16, :128], "tp", 1)]

    kept, leaving = out[2], out[3:]
    half_way = leaving[0].shape[0]
    for i, mine in enumerate(leaving):
        come = hop(mine, "tp", 1)
        total = kept[i * half_way : (i + 1) * half_way].astype(F32) + come.astype(F32)
        total = total.astype(BF16)
        for m in range(half_way):
            k = i * half_way + m
            terms[names[k // pairs][k % pairs]] = total[m]

    keep = {}
    for e in range(n_ep // 2):
        for y in range(pairs):
            keep[e, y] = terms[names[e][y]].astype(F32)
    top = n_ep // 4
    for e in range(n_ep // 2 - 1, top, -1):
        for y in range(pairs):
            if y and e > top:
                keep[e - top, y] += hop(keep[e, y].astype(BF16), "ep", top).astype(F32)
            elif e > top:
                keep[top, 0] += hop(keep[e, y].astype(BF16), "ep", e - top).astype(F32)
    for y in range(1, pairs):
        keep[top, 0] += hop(keep[top, y].astype(BF16), "tp", 2 * y).astype(F32)
    total = keep[0, 0]
    for e in range(top + 1):
        for y in range(pairs if e < top else 1):
            if e or y:
                sums = keep[e, y].astype(BF16)
                total = total + leap(sums, e, 2 * y).astype(F32)
    in_grad = total.astype(BF16)

    grad_in, grad_out = far_call(where, pieces[n_ep // 2 :], w_in, w_out, tok, near)
    return in_grad, grad_in.reshape(1, 2, ffl, -1), grad_out[None]


def solution(mesh):
    return jax.shard_map(
        body,
        mesh=mesh,
        in_specs=(
            P("ep", "tp"),
            P("ep", "tp"),
            P("ep", None),
            P("ep", None),
            P("ep", None, "tp", None),
            P("ep", "tp", None),
        ),
        out_specs=(P("ep", "tp"), P("ep", None, "tp", None), P("ep", "tp", None)),
        check_vma=False,
    )
```

```python
import functools

import jax
import jax.numpy as jnp
from jax import lax
from jax.experimental import pallas as pl
from jax.experimental.pallas import tpu as pltpu
from jax.sharding import PartitionSpec as P

BF16 = jnp.bfloat16
F32 = jnp.float32
VMEM_LIMIT = 58 * 1024 * 1024
SLOTS = 3
SHRINK = 1.0 / 64.0


def hop(block, axis, bit):
    count = lax.axis_size(axis)
    return lax.ppermute(block, axis, [(i, i ^ bit) for i in range(count)])


def leap(block, ep, tp):
    wide, count = lax.axis_size("tp"), lax.axis_size("ep") * lax.axis_size("tp")
    apart = ep * wide + tp
    return lax.ppermute(block, ("ep", "tp"), [(i, i ^ apart) for i in range(count)])


def after(value, *others):
    return lax.optimization_barrier((value,) + others)[0] if others else value


def bits_of(number, letter, skip=0):
    return [f"{letter}{i}" for i in range(skip, number.bit_length() - 1)]


class Lanes:
    def __init__(self, depth):
        self.depth = depth
        self.sent = {}

    def send(self, block, bit, *others):
        queue = self.sent.setdefault(bit, [])
        ready = list(others)
        if bit != "t0":
            ready += queue[-self.depth : len(queue) - self.depth + 1]
        axis = "ep" if bit[0] == "e" else "tp"
        queue.append(hop(after(block, *ready), axis, 1 << int(bit[1:])))
        return queue[-1]


def gather_plan(n_ep, n_tp):
    if (n_ep, n_tp) == (8, 4):
        x, n, f, y = "e0", "e1", "e2", "t1"
        near = (x, n), (y, n), (x, y, n)
        far = (x, f), (y, f), (n, f)
        return [
            ((x,), x, 2), ((y,), y, 2), ((n,), n, 2), ((f,), f, 2),
            ((x, y), x, 0), ((x, y), y, 1),
            ((x, n), x, 2, (f,)), ((y, n), y, 2, (f,)), ((x, y, n), n, 2, (f,)),
            ((x, f), x, 2, *near), ((y, f), y, 2, *near), ((n, f), n, 2, *near),
            ((x, y, f), x, 2, *far, 0), ((y, n, f), y, 2, *far, 0), ((x, n, f), n, 2, *far, 0),
            ((x, y, n, f), x, 0), ((x, y, n, f), y, 1),
        ]
    bits = bits_of(n_ep, "e") + bits_of(n_tp, "t", 1)
    plan = []
    for i, bit in enumerate(bits):
        for low in range(1 << i):
            below = tuple(b for j, b in enumerate(bits[:i]) if low >> j & 1)
            plan.append((below + (bit,), bit, 2))
    return plan


def name_of(ep, tp):
    names = [f"e{i}" for i in range(ep.bit_length()) if ep >> i & 1]
    names += [f"t{i + 1}" for i in range(tp.bit_length()) if tp >> i & 1]
    return frozenset(names)


def rows_of(refs, tok):
    if len(refs) == 1:
        return refs[0].at[0:tok], refs[0].at[tok : 2 * tok], refs[0].at[2 * tok : 2 * tok + 16]
    return refs[0], refs[1].at[0:tok], refs[1].at[tok : tok + 16]


def weights_row(ref, expert, tok):
    width = ref.shape[1]
    per = width // tok
    table = ref[...].astype(F32)
    lines = lax.broadcasted_iota(jnp.int32, table.shape, 0)
    lanes = lax.broadcasted_iota(jnp.int32, table.shape, 1)
    table = jnp.where((lines == expert // per) & (lanes // tok == expert % per), table, 0.0)
    line = jnp.sum(table, axis=0, keepdims=True)
    return functools.reduce(jnp.add, [line[:, i * tok : (i + 1) * tok] for i in range(per)])


def rows_kernel(n_tp, sizes, part, where_ref, win_ref, wout_ref, *refs):
    blocks = len(sizes) // n_tp
    pieces = [[] for _ in range(blocks)]
    for k, size in enumerate(sizes):
        pieces[k // n_tp].append(refs[:size])
        refs = refs[size:]
    if part:
        dadb_ref, hid_ref, *part_refs = refs[:5]
        refs = refs[5:]
    else:
        dadb_ref, hid_ref, *refs = refs
    xs, gs, ps, wi, wo, acc, sems, psems, wsems = refs
    ffl = hid_ref.shape[0]
    tok = hid_ref.shape[1] // blocks
    width = wout_ref.shape[1] // n_tp

    def column(d):
        return pl.ds(pl.multiple_of((where_ref[0] ^ d) * width, width), width)

    copies = []
    for d in range(n_tp):
        mine = []
        for j in range(blocks):
            x, g, _ = rows_of(pieces[j][d], tok)
            into = pl.ds(j * tok, tok)
            mine.append(pltpu.make_async_copy(x, xs.at[d, into], sems.at[d, j, 0]))
            mine.append(pltpu.make_async_copy(g, gs.at[d, into], sems.at[d, j, 1]))
        mine.append(pltpu.make_async_copy(win_ref.at[:, column(d)], wi.at[d], wsems.at[d, 0]))
        mine.append(pltpu.make_async_copy(wout_ref.at[:, column(d)], wo.at[d], wsems.at[d, 1]))
        copies.append(mine)
    tables = []
    for j in range(blocks):
        table = rows_of(pieces[j][0], tok)[2]
        tables.append(pltpu.make_async_copy(table, ps.at[j], psems.at[j]))
        tables[j].start()

    for copy in copies[0] + copies[1]:
        copy.start()
    last = (((1,), (1,)), ((), ()))
    for d in range(n_tp):
        for copy in copies[d]:
            copy.wait()
        for copy in copies[d + 2] if d + 2 < n_tp else ():
            copy.start()
        x = xs[d]
        g = gs[d] * jnp.asarray(SHRINK, BF16)
        ab = lax.dot_general(wi[d], x, last, preferred_element_type=F32)
        h = lax.dot_general(wo[d], g, last, preferred_element_type=F32)
        if d == 0:
            acc[pl.ds(0, 2 * ffl)] = ab
            acc[pl.ds(2 * ffl, ffl)] = h
        else:
            acc[pl.ds(0, 2 * ffl)] += ab
            acc[pl.ds(2 * ffl, ffl)] += h
    scale = []
    for j in range(blocks):
        tables[j].wait()
        first = weights_row(ps.at[j], where_ref[1], tok)
        scale.append(first + weights_row(ps.at[j], where_ref[2], tok))
    scale = jnp.concatenate(scale, axis=1)
    a = acc[pl.ds(0, ffl)]
    b = acc[pl.ds(ffl, ffl)]
    named = scale > 0.0
    dh = acc[pl.ds(2 * ffl, ffl)] * (scale * (1.0 / SHRINK))
    sig = jax.nn.sigmoid(a)
    silu = a * sig
    da = dh * b * sig * (1.0 + a * (1.0 - sig))
    dadb_ref[pl.ds(0, ffl)] = jnp.where(named, da, 0.0).astype(BF16)
    dadb_ref[pl.ds(ffl, ffl)] = jnp.where(named, dh * silu, 0.0).astype(BF16)
    hid_ref[...] = jnp.where(named, (0.5 * scale) * (silu * b), 0.0).astype(BF16)
    if part:
        lhs = dadb_ref[...].T
        for d in range(n_tp):
            out = jnp.dot(lhs, wi[d], preferred_element_type=F32).astype(BF16)
            for j in range(blocks):
                piece, half = j * (n_tp // 2) + d // 2, blocks * n_tp // 4
                into = part_refs[1 + piece // half] if d % 2 else part_refs[0]
                into[piece % half if d % 2 else piece] = out[j * tok : (j + 1) * tok]


def rows_call(part, where, pieces, w_in, w_out, tok):
    n_tp = len(pieces[0])
    flat = [piece for block in pieces for piece in block]
    sizes = [len(piece) for piece in flat]
    arrays = [array for piece in flat for array in piece]
    blocks = len(pieces)
    rows, width = blocks * tok, arrays[0].shape[1]
    ffl = w_out.shape[0]
    outs = [
        jax.ShapeDtypeStruct((2 * ffl, rows), BF16),
        jax.ShapeDtypeStruct((ffl, rows), BF16),
    ]
    if part:
        outs += [
            jax.ShapeDtypeStruct((blocks * n_tp // k, tok, width), BF16) for k in (2, 4, 4)
        ]
    vmem = pl.BlockSpec(memory_space=pltpu.VMEM)
    hbm = pl.BlockSpec(memory_space=pltpu.HBM)
    return pl.pallas_call(
        functools.partial(rows_kernel, n_tp, sizes, part),
        out_shape=outs,
        in_specs=[pl.BlockSpec(memory_space=pltpu.SMEM)] + [hbm] * (2 + len(arrays)),
        out_specs=[vmem] * len(outs),
        scratch_shapes=[
            pltpu.VMEM((n_tp, rows, width), BF16),
            pltpu.VMEM((n_tp, rows, width), BF16),
            pltpu.VMEM((blocks, 16, width), BF16),
            pltpu.VMEM((n_tp, 2 * ffl, width), BF16),
            pltpu.VMEM((n_tp, ffl, width), BF16),
            pltpu.VMEM((3 * ffl, rows), F32),
            pltpu.SemaphoreType.DMA((n_tp, blocks, 2)),
            pltpu.SemaphoreType.DMA((blocks,)),
            pltpu.SemaphoreType.DMA((n_tp, 2)),
        ],
        compiler_params=pltpu.CompilerParams(vmem_limit_bytes=VMEM_LIMIT),
        cost_estimate=pl.CostEstimate(
            flops=2 * rows * ffl * n_tp * width * (5 if part else 3),
            bytes_accessed=2 * (3 * ffl + 2 * rows) * n_tp * width,
            transcendentals=rows * ffl,
        ),
        name="rows",
    )(where, w_in, w_out, *arrays)


def far_kernel(n_tp, sizes, where_ref, win_ref, wout_ref, *refs):
    blocks = len(sizes) // n_tp
    pieces = [[] for _ in range(blocks)]
    for k, size in enumerate(sizes):
        pieces[k // n_tp].append(refs[:size])
        refs = refs[size:]
    base, refs = refs[:2], refs[2:]
    gin_ref, gout_ref, xs, gs, ps, wi, wo, acc, dadb_ref, hid_ref, bi, bo, oi, oo, *refs = refs
    sems, psems, wsems, bsems, osems = refs
    ffl = hid_ref.shape[0]
    tok = hid_ref.shape[1] // blocks
    width = wout_ref.shape[1] // n_tp

    def column(d):
        return pl.ds(pl.multiple_of((where_ref[0] ^ d) * width, width), width)

    copies = []
    for d in range(n_tp):
        mine = []
        for j in range(blocks):
            x, g, _ = rows_of(pieces[j][d], tok)
            into = pl.ds(j * tok, tok)
            mine.append(pltpu.make_async_copy(x, xs.at[d, into], sems.at[d, j, 0]))
            mine.append(pltpu.make_async_copy(g, gs.at[d, into], sems.at[d, j, 1]))
        mine.append(pltpu.make_async_copy(win_ref.at[:, column(d)], wi.at[d], wsems.at[d, 0]))
        mine.append(pltpu.make_async_copy(wout_ref.at[:, column(d)], wo.at[d], wsems.at[d, 1]))
        copies.append(mine)
    tables = []
    for j in range(blocks):
        table = rows_of(pieces[j][0], tok)[2]
        tables.append(pltpu.make_async_copy(table, ps.at[j], psems.at[j]))
        tables[j].start()

    for copy in copies[0] + copies[1]:
        copy.start()
    last = (((1,), (1,)), ((), ()))
    for d in range(n_tp):
        for copy in copies[d]:
            copy.wait()
        for copy in copies[d + 2] if d + 2 < n_tp else ():
            copy.start()
        if d == n_tp - 2:
            added = [pltpu.make_async_copy(base[0], bi, bsems.at[0])]
            added.append(pltpu.make_async_copy(base[1], bo, bsems.at[1]))
            for copy in added:
                copy.start()
        x = xs[d]
        g = gs[d] * jnp.asarray(SHRINK, BF16)
        ab = lax.dot_general(wi[d], x, last, preferred_element_type=F32)
        h = lax.dot_general(wo[d], g, last, preferred_element_type=F32)
        if d == 0:
            acc[pl.ds(0, 2 * ffl)] = ab
            acc[pl.ds(2 * ffl, ffl)] = h
        else:
            acc[pl.ds(0, 2 * ffl)] += ab
            acc[pl.ds(2 * ffl, ffl)] += h
    scale = []
    for j in range(blocks):
        tables[j].wait()
        first = weights_row(ps.at[j], where_ref[1], tok)
        scale.append(first + weights_row(ps.at[j], where_ref[2], tok))
    scale = jnp.concatenate(scale, axis=1)
    a = acc[pl.ds(0, ffl)]
    b = acc[pl.ds(ffl, ffl)]
    named = scale > 0.0
    dh = acc[pl.ds(2 * ffl, ffl)] * (scale * (1.0 / SHRINK))
    sig = jax.nn.sigmoid(a)
    silu = a * sig
    da = dh * b * sig * (1.0 + a * (1.0 - sig))
    dadb_ref[pl.ds(0, ffl)] = jnp.where(named, da, 0.0).astype(BF16)
    dadb_ref[pl.ds(ffl, ffl)] = jnp.where(named, dh * silu, 0.0).astype(BF16)
    hid_ref[...] = jnp.where(named, (0.5 * scale) * (silu * b), 0.0).astype(BF16)
    for copy in added:
        copy.wait()
    tile = oi.shape[2]
    tiles = width // tile
    leaving = {}
    for k in range(n_tp * tiles):
        slot, d, cols = k % 2, k // tiles, pl.ds(k % tiles * tile, tile)
        start = (where_ref[0] ^ d) * width + k % tiles * tile
        here = pl.ds(pl.multiple_of(start, tile), tile)
        for copy in leaving.pop(k - 2, ()):
            copy.wait()
        gi = jnp.dot(dadb_ref[...], xs[d, :, cols], preferred_element_type=F32)
        go = 2.0 * jnp.dot(hid_ref[...], gs[d, :, cols], preferred_element_type=F32)
        oi[slot] = (gi + bi[:, here].astype(F32)).astype(BF16)
        oo[slot] = (go + bo[:, here].astype(F32)).astype(BF16)
        leaving[k] = (
            pltpu.make_async_copy(oi.at[slot], gin_ref.at[:, here], osems.at[slot, 0]),
            pltpu.make_async_copy(oo.at[slot], gout_ref.at[:, here], osems.at[slot, 1]),
        )
        for copy in leaving[k]:
            copy.start()
    for copies in leaving.values():
        for copy in copies:
            copy.wait()


def far_call(where, pieces, w_in, w_out, tok, base):
    n_tp = len(pieces[0])
    flat = [piece for block in pieces for piece in block]
    sizes = [len(piece) for piece in flat]
    arrays = [array for piece in flat for array in piece]
    blocks = len(pieces)
    rows, width = blocks * tok, arrays[0].shape[1]
    ffl, depth = w_out.shape
    tile = width
    hbm = pl.BlockSpec(memory_space=pltpu.HBM)
    return pl.pallas_call(
        functools.partial(far_kernel, n_tp, sizes),
        out_shape=[
            jax.ShapeDtypeStruct((2 * ffl, depth), BF16),
            jax.ShapeDtypeStruct((ffl, depth), BF16),
        ],
        in_specs=[pl.BlockSpec(memory_space=pltpu.SMEM)] + [hbm] * (4 + len(arrays)),
        out_specs=[hbm, hbm],
        scratch_shapes=[
            pltpu.VMEM((n_tp, rows, width), BF16),
            pltpu.VMEM((n_tp, rows, width), BF16),
            pltpu.VMEM((blocks, 16, width), BF16),
            pltpu.VMEM((n_tp, 2 * ffl, width), BF16),
            pltpu.VMEM((n_tp, ffl, width), BF16),
            pltpu.VMEM((3 * ffl, rows), F32),
            pltpu.VMEM((2 * ffl, rows), BF16),
            pltpu.VMEM((ffl, rows), BF16),
            pltpu.VMEM((2 * ffl, depth), BF16),
            pltpu.VMEM((ffl, depth), BF16),
            pltpu.VMEM((2, 2 * ffl, tile), BF16),
            pltpu.VMEM((2, ffl, tile), BF16),
            pltpu.SemaphoreType.DMA((n_tp, blocks, 2)),
            pltpu.SemaphoreType.DMA((blocks,)),
            pltpu.SemaphoreType.DMA((n_tp, 2)),
            pltpu.SemaphoreType.DMA((2,)),
            pltpu.SemaphoreType.DMA((2, 2)),
        ],
        compiler_params=pltpu.CompilerParams(vmem_limit_bytes=VMEM_LIMIT),
        cost_estimate=pl.CostEstimate(
            flops=12 * rows * ffl * depth,
            bytes_accessed=2 * (9 * ffl + 2 * rows) * depth,
            transcendentals=rows * ffl,
        ),
        name="far",
    )(where, w_in, w_out, *arrays, *base)


def grads_kernel(steps, sizes, added, filled, where_ref, dadb_ref, hid_ref, *refs):
    pieces = []
    tok = hid_ref.shape[1] * len(steps) // len(sizes)
    for size in sizes:
        pieces.append(rows_of(refs[:size], tok))
        refs = refs[size:]
    base, refs = (refs[:2], refs[2:]) if added else ((), refs)
    gin_ref, gout_ref, xs, gs, oi, oo, bi, bo, sems, bsems, osems = refs[2 if filled else 0 :]
    width = pieces[0][0].shape[1]
    slots, _, tile = xs.shape
    tiles = width // tile
    total = len(steps) * tiles

    def column(k):
        start = (where_ref[0] ^ steps[k // tiles]) * width + k % tiles * tile
        return pl.ds(pl.multiple_of(start, tile), tile)

    def fetch(k):
        slot, cols = k % slots, pl.ds(k % tiles * tile, tile)
        copies = []
        for i, (x, g, _) in enumerate(pieces[k // tiles :: len(steps)]):
            into = pl.ds(i * tok, tok)
            copies.append(pltpu.make_async_copy(x.at[:, cols], xs.at[slot, into], sems.at[slot, i, 0]))
            copies.append(pltpu.make_async_copy(g.at[:, cols], gs.at[slot, into], sems.at[slot, i, 1]))
        for i, (src, dst) in enumerate(zip(base, (bi, bo))):
            copies.append(pltpu.make_async_copy(src.at[:, column(k)], dst.at[slot], bsems.at[slot, i]))
        for copy in copies:
            copy.start()
        return copies

    coming = [fetch(k) for k in range(min(slots - 1, total))]
    leaving = {}
    for k in range(total):
        slot = k % slots
        if k + slots - 1 < total:
            coming.append(fetch(k + slots - 1))
        for copy in coming[k]:
            copy.wait()
        for copy in leaving.pop(k - slots, ()):
            copy.wait()
        gi = jnp.dot(dadb_ref[...], xs[slot], preferred_element_type=F32)
        go = 2.0 * jnp.dot(hid_ref[...], gs[slot], preferred_element_type=F32)
        if added:
            gi = gi + bi[slot].astype(F32)
            go = go + bo[slot].astype(F32)
        oi[slot] = gi.astype(BF16)
        oo[slot] = go.astype(BF16)
        leaving[k] = (
            pltpu.make_async_copy(oi.at[slot], gin_ref.at[:, column(k)], osems.at[slot, 0]),
            pltpu.make_async_copy(oo.at[slot], gout_ref.at[:, column(k)], osems.at[slot, 1]),
        )
        for copy in leaving[k]:
            copy.start()
    for copies in leaving.values():
        for copy in copies:
            copy.wait()


def grads_call(where, dadb, hid, pieces, steps, base=(), filled=()):
    n_tp = len(pieces[0])
    flat = [block[d] for block in pieces for d in steps]
    sizes = [len(piece) for piece in flat]
    arrays = [array for piece in flat for array in piece]
    width = arrays[0].shape[1]
    ffl, rows = hid.shape
    depth = n_tp * width
    tile = min(512, width)
    vmem = pl.BlockSpec(memory_space=pltpu.VMEM)
    hbm = pl.BlockSpec(memory_space=pltpu.HBM)
    operands = [where, dadb, hid, *arrays, *base, *filled]
    return pl.pallas_call(
        functools.partial(grads_kernel, steps, sizes, len(base) > 0, len(filled) > 0),
        out_shape=[
            jax.ShapeDtypeStruct((2 * ffl, depth), BF16),
            jax.ShapeDtypeStruct((ffl, depth), BF16),
        ],
        in_specs=[pl.BlockSpec(memory_space=pltpu.SMEM), vmem, vmem]
        + [hbm] * (len(operands) - 3),
        out_specs=[hbm, hbm],
        input_output_aliases={len(operands) - 2: 0, len(operands) - 1: 1} if filled else {},
        scratch_shapes=[
            pltpu.VMEM((SLOTS, rows, tile), BF16),
            pltpu.VMEM((SLOTS, rows, tile), BF16),
            pltpu.VMEM((SLOTS, 2 * ffl, tile), BF16),
            pltpu.VMEM((SLOTS, ffl, tile), BF16),
            pltpu.VMEM((SLOTS, 2 * ffl, tile), BF16),
            pltpu.VMEM((SLOTS, ffl, tile), BF16),
            pltpu.SemaphoreType.DMA((SLOTS, len(pieces), 2)),
            pltpu.SemaphoreType.DMA((SLOTS, 2)),
            pltpu.SemaphoreType.DMA((SLOTS, 2)),
        ],
        compiler_params=pltpu.CompilerParams(vmem_limit_bytes=VMEM_LIMIT),
        cost_estimate=pl.CostEstimate(
            flops=6 * rows * ffl * len(steps) * width,
            bytes_accessed=2 * (3 * ffl + 2 * rows) * len(steps) * width,
            transcendentals=0,
        ),
        name="grads",
    )(*operands)


def own_rows(tokens, out_grad, routes, probs, n_ep):
    tok, width = tokens.shape
    copies = jnp.arange(n_ep, dtype=jnp.int32)[:, None, None]
    table = jnp.sum(jnp.where(routes[None] == copies, probs[None], 0), axis=2).astype(BF16)
    table = table.reshape(n_ep * tok // width, width)
    table = jnp.pad(table, ((0, 16 - table.shape[0]), (0, 0)))
    return jnp.concatenate([tokens, out_grad, table])


def body(tokens, out_grad, routes, probs, w_in, w_out):
    n_ep, n_tp = lax.axis_size("ep"), lax.axis_size("tp")
    pairs = n_tp // 2
    ffl = w_out.shape[1]
    w_in = w_in.reshape(2 * ffl, w_in.shape[3])
    w_out = w_out[0]
    tok = tokens.shape[0]
    expert = lax.axis_index("ep") % (n_ep // 2)
    where = jnp.stack([lax.axis_index("tp"), expert, expert + n_ep // 2]).astype(jnp.int32)

    lanes = Lanes(1)
    have = {frozenset(): {2: own_rows(tokens, out_grad, routes, probs, n_ep)}}

    def held(name, part):
        parts = have[name]
        if part not in parts:
            if part == 2:
                parts[2] = jnp.concatenate([parts[0], parts[1]])
            else:
                parts[part] = parts[2][:tok] if part == 0 else parts[2][tok:]
        return parts[part]

    def arrays(name):
        parts = have[name]
        return (parts[2],) if 2 in parts else (parts[0], parts[1])

    names = [[name_of(e, y) for y in range(pairs)] for e in range(n_ep)]
    half_of = {name: 2 * e // n_ep for e in range(n_ep) for name in names[e]}
    missing = [n_ep * pairs - 2, n_ep * pairs]
    pieces = [None] * n_ep
    done = []
    terms = {}
    other = {frozenset(): (lanes.send(have[frozenset()][2], "t0"),)}
    plan = gather_plan(n_ep, n_tp)
    for target, bit, part, *first in plan:
        target = frozenset(target)
        before = []
        for what in first:
            before.append(done[what] if isinstance(what, int) else have[frozenset(what)][2])
        have.setdefault(target, {})[part] = lanes.send(held(target - {bit}, part), bit, *before)
        if 2 in have[target] or len(have[target]) == 2:
            other[target] = tuple(lanes.send(array, "t0") for array in arrays(target))
        half = half_of[target]
        missing[half] -= 2 if part == 2 else 1
        if missing[half]:
            continue
        blocks = range(half * n_ep // 2, (half + 1) * n_ep // 2)
        for e in blocks:
            pieces[e] = [
                arrays(names[e][d // 2]) if d % 2 == 0 else other[names[e][d // 2]]
                for d in range(n_tp)
            ]
        mine = pieces[blocks[0] : blocks[-1] + 1]
        if half == 0:
            out = rows_call(True, where, mine, w_in, w_out, tok)
            near = grads_call(where, out[0], out[1], mine, list(range(n_tp)))
            done += [out[1], hop(near[1][:16, :128], "tp", 1)]

    kept, leaving = out[2], out[3:]
    half_way = leaving[0].shape[0]
    for i, mine in enumerate(leaving):
        come = hop(mine, "tp", 1)
        total = kept[i * half_way : (i + 1) * half_way].astype(F32) + come.astype(F32)
        total = total.astype(BF16)
        for m in range(half_way):
            k = i * half_way + m
            terms[names[k // pairs][k % pairs]] = total[m]

    keep = {}
    for e in range(n_ep // 2):
        for y in range(pairs):
            keep[e, y] = terms[names[e][y]].astype(F32)
    top = n_ep // 4
    for e in range(n_ep // 2 - 1, top, -1):
        for y in range(pairs):
            if y and e > top:
                keep[e - top, y] += hop(keep[e, y].astype(BF16), "ep", top).astype(F32)
            elif e > top:
                keep[top, 0] += hop(keep[e, y].astype(BF16), "ep", e - top).astype(F32)
    for y in range(1, pairs):
        keep[top, 0] += hop(keep[top, y].astype(BF16), "tp", 2 * y).astype(F32)
    total = keep[0, 0]
    for e in range(top + 1):
        for y in range(pairs if e < top else 1):
            if e or y:
                sums = keep[e, y].astype(BF16)
                total = total + leap(sums, e, 2 * y).astype(F32)
    in_grad = total.astype(BF16)

    grad_in, grad_out = far_call(where, pieces[n_ep // 2 :], w_in, w_out, tok, near)
    return in_grad, grad_in.reshape(1, 2, ffl, -1), grad_out[None]


def solution(mesh):
    return jax.shard_map(
        body,
        mesh=mesh,
        in_specs=(
            P("ep", "tp"),
            P("ep", "tp"),
            P("ep", None),
            P("ep", None),
            P("ep", None, "tp", None),
            P("ep", "tp", None),
        ),
        out_specs=(P("ep", "tp"), P("ep", None, "tp", None), P("ep", "tp", None)),
        check_vma=False,
    )
```

```python
import functools

import jax
import jax.numpy as jnp
from jax import lax
from jax.experimental import pallas as pl
from jax.experimental.pallas import tpu as pltpu
from jax.sharding import PartitionSpec as P

BF16 = jnp.bfloat16
F32 = jnp.float32
VMEM_LIMIT = 58 * 1024 * 1024
SLOTS = 3
SHRINK = 1.0 / 64.0


def hop(block, axis, bit):
    count = lax.axis_size(axis)
    return lax.ppermute(block, axis, [(i, i ^ bit) for i in range(count)])


def leap(block, ep, tp):
    wide, count = lax.axis_size("tp"), lax.axis_size("ep") * lax.axis_size("tp")
    apart = ep * wide + tp
    return lax.ppermute(block, ("ep", "tp"), [(i, i ^ apart) for i in range(count)])


def after(value, *others):
    return lax.optimization_barrier((value,) + others)[0] if others else value


def bits_of(number, letter, skip=0):
    return [f"{letter}{i}" for i in range(skip, number.bit_length() - 1)]


class Lanes:
    def __init__(self, depth):
        self.depth = depth
        self.sent = {}

    def send(self, block, bit, *others):
        queue = self.sent.setdefault(bit, [])
        ready = list(others)
        if bit != "t0":
            ready += queue[-self.depth : len(queue) - self.depth + 1]
        axis = "ep" if bit[0] == "e" else "tp"
        queue.append(hop(after(block, *ready), axis, 1 << int(bit[1:])))
        return queue[-1]


def gather_plan(n_ep, n_tp):
    if (n_ep, n_tp) == (8, 4):
        x, n, f, y = "e0", "e1", "e2", "t1"
        near = (x, n), (y, n), (x, y, n)
        far = (x, f), (y, f), (n, f)
        return [
            ((x,), x, 2), ((y,), y, 2), ((n,), n, 2), ((f,), f, 2),
            ((x, y), x, 0), ((x, y), y, 1),
            ((x, n), x, 2, (f,)), ((y, n), y, 2, (f,)), ((x, y, n), n, 2, (f,)),
            ((x, f), x, 2, *near), ((y, f), y, 2, *near), ((n, f), n, 2, *near),
            ((x, y, f), x, 2, *far, 0), ((y, n, f), y, 2, *far, 0), ((x, n, f), n, 2, *far, 0),
            ((x, y, n, f), x, 0), ((x, y, n, f), y, 1),
        ]
    bits = bits_of(n_ep, "e") + bits_of(n_tp, "t", 1)
    plan = []
    for i, bit in enumerate(bits):
        for low in range(1 << i):
            below = tuple(b for j, b in enumerate(bits[:i]) if low >> j & 1)
            plan.append((below + (bit,), bit, 2))
    return plan


def name_of(ep, tp):
    names = [f"e{i}" for i in range(ep.bit_length()) if ep >> i & 1]
    names += [f"t{i + 1}" for i in range(tp.bit_length()) if tp >> i & 1]
    return frozenset(names)


def rows_of(refs, tok):
    if len(refs) == 1:
        return refs[0].at[0:tok], refs[0].at[tok : 2 * tok], refs[0].at[2 * tok : 2 * tok + 16]
    return refs[0], refs[1].at[0:tok], refs[1].at[tok : tok + 16]


def weights_row(ref, expert, tok):
    width = ref.shape[1]
    per = width // tok
    table = ref[...].astype(F32)
    lines = lax.broadcasted_iota(jnp.int32, table.shape, 0)
    lanes = lax.broadcasted_iota(jnp.int32, table.shape, 1)
    table = jnp.where((lines == expert // per) & (lanes // tok == expert % per), table, 0.0)
    line = jnp.sum(table, axis=0, keepdims=True)
    return functools.reduce(jnp.add, [line[:, i * tok : (i + 1) * tok] for i in range(per)])


def rows_kernel(n_tp, sizes, part, where_ref, win_ref, wout_ref, *refs):
    blocks = len(sizes) // n_tp
    pieces = [[] for _ in range(blocks)]
    for k, size in enumerate(sizes):
        pieces[k // n_tp].append(refs[:size])
        refs = refs[size:]
    if part:
        dadb_ref, hid_ref, *part_refs = refs[:5]
        refs = refs[5:]
    else:
        dadb_ref, hid_ref, *refs = refs
    xs, gs, ps, wi, wo, acc, sems, psems, wsems = refs
    ffl = hid_ref.shape[0]
    tok = hid_ref.shape[1] // blocks
    width = wout_ref.shape[1] // n_tp

    def column(d):
        return pl.ds(pl.multiple_of((where_ref[0] ^ d) * width, width), width)

    copies = []
    for d in range(n_tp):
        mine = []
        for j in range(blocks):
            x, g, _ = rows_of(pieces[j][d], tok)
            into = pl.ds(j * tok, tok)
            mine.append(pltpu.make_async_copy(x, xs.at[d, into], sems.at[d, j, 0]))
            mine.append(pltpu.make_async_copy(g, gs.at[d, into], sems.at[d, j, 1]))
        mine.append(pltpu.make_async_copy(win_ref.at[:, column(d)], wi.at[d], wsems.at[d, 0]))
        mine.append(pltpu.make_async_copy(wout_ref.at[:, column(d)], wo.at[d], wsems.at[d, 1]))
        copies.append(mine)
    tables = []
    for j in range(blocks):
        table = rows_of(pieces[j][0], tok)[2]
        tables.append(pltpu.make_async_copy(table, ps.at[j], psems.at[j]))
        tables[j].start()

    for copy in copies[0] + copies[1]:
        copy.start()
    last = (((1,), (1,)), ((), ()))
    for d in range(n_tp):
        for copy in copies[d]:
            copy.wait()
        for copy in copies[d + 2] if d + 2 < n_tp else ():
            copy.start()
        x = xs[d]
        g = gs[d] * jnp.asarray(SHRINK, BF16)
        ab = lax.dot_general(wi[d], x, last, preferred_element_type=F32)
        h = lax.dot_general(wo[d], g, last, preferred_element_type=F32)
        if d == 0:
            acc[pl.ds(0, 2 * ffl)] = ab
            acc[pl.ds(2 * ffl, ffl)] = h
        else:
            acc[pl.ds(0, 2 * ffl)] += ab
            acc[pl.ds(2 * ffl, ffl)] += h
    scale = []
    for j in range(blocks):
        tables[j].wait()
        first = weights_row(ps.at[j], where_ref[1], tok)
        scale.append(first + weights_row(ps.at[j], where_ref[2], tok))
    scale = jnp.concatenate(scale, axis=1)
    a = acc[pl.ds(0, ffl)]
    b = acc[pl.ds(ffl, ffl)]
    named = scale > 0.0
    dh = acc[pl.ds(2 * ffl, ffl)] * (scale * (1.0 / SHRINK))
    sig = jax.nn.sigmoid(a)
    silu = a * sig
    da = dh * b * sig * (1.0 + a * (1.0 - sig))
    dadb_ref[pl.ds(0, ffl)] = jnp.where(named, da, 0.0).astype(BF16)
    dadb_ref[pl.ds(ffl, ffl)] = jnp.where(named, dh * silu, 0.0).astype(BF16)
    hid_ref[...] = jnp.where(named, (0.5 * scale) * (silu * b), 0.0).astype(BF16)
    if part:
        lhs = dadb_ref[...].T
        for d in range(n_tp):
            out = jnp.dot(lhs, wi[d], preferred_element_type=F32).astype(BF16)
            for j in range(blocks):
                piece, half = j * (n_tp // 2) + d // 2, blocks * n_tp // 4
                into = part_refs[1 + piece // half] if d % 2 else part_refs[0]
                into[piece % half if d % 2 else piece] = out[j * tok : (j + 1) * tok]


def rows_call(part, where, pieces, w_in, w_out, tok):
    n_tp = len(pieces[0])
    flat = [piece for block in pieces for piece in block]
    sizes = [len(piece) for piece in flat]
    arrays = [array for piece in flat for array in piece]
    blocks = len(pieces)
    rows, width = blocks * tok, arrays[0].shape[1]
    ffl = w_out.shape[0]
    outs = [
        jax.ShapeDtypeStruct((2 * ffl, rows), BF16),
        jax.ShapeDtypeStruct((ffl, rows), BF16),
    ]
    if part:
        outs += [
            jax.ShapeDtypeStruct((blocks * n_tp // k, tok, width), BF16) for k in (2, 4, 4)
        ]
    vmem = pl.BlockSpec(memory_space=pltpu.VMEM)
    hbm = pl.BlockSpec(memory_space=pltpu.HBM)
    return pl.pallas_call(
        functools.partial(rows_kernel, n_tp, sizes, part),
        out_shape=outs,
        in_specs=[pl.BlockSpec(memory_space=pltpu.SMEM)] + [hbm] * (2 + len(arrays)),
        out_specs=[vmem] * len(outs),
        scratch_shapes=[
            pltpu.VMEM((n_tp, rows, width), BF16),
            pltpu.VMEM((n_tp, rows, width), BF16),
            pltpu.VMEM((blocks, 16, width), BF16),
            pltpu.VMEM((n_tp, 2 * ffl, width), BF16),
            pltpu.VMEM((n_tp, ffl, width), BF16),
            pltpu.VMEM((3 * ffl, rows), F32),
            pltpu.SemaphoreType.DMA((n_tp, blocks, 2)),
            pltpu.SemaphoreType.DMA((blocks,)),
            pltpu.SemaphoreType.DMA((n_tp, 2)),
        ],
        compiler_params=pltpu.CompilerParams(vmem_limit_bytes=VMEM_LIMIT),
        cost_estimate=pl.CostEstimate(
            flops=2 * rows * ffl * n_tp * width * (5 if part else 3),
            bytes_accessed=2 * (3 * ffl + 2 * rows) * n_tp * width,
            transcendentals=rows * ffl,
        ),
        name="rows",
    )(where, w_in, w_out, *arrays)


def far_kernel(n_tp, sizes, where_ref, win_ref, wout_ref, *refs):
    blocks = len(sizes) // n_tp
    pieces = [[] for _ in range(blocks)]
    for k, size in enumerate(sizes):
        pieces[k // n_tp].append(refs[:size])
        refs = refs[size:]
    base, refs = refs[:2], refs[2:]
    gin_ref, gout_ref, xs, gs, ps, wi, wo, acc, dadb_ref, hid_ref, bi, bo, oi, oo, *refs = refs
    sems, psems, wsems, bsems, osems = refs
    ffl = hid_ref.shape[0]
    tok = hid_ref.shape[1] // blocks
    width = wout_ref.shape[1] // n_tp

    def column(d):
        return pl.ds(pl.multiple_of((where_ref[0] ^ d) * width, width), width)

    copies = []
    for d in range(n_tp):
        mine = []
        for j in range(blocks):
            x, g, _ = rows_of(pieces[j][d], tok)
            into = pl.ds(j * tok, tok)
            mine.append(pltpu.make_async_copy(x, xs.at[d, into], sems.at[d, j, 0]))
            mine.append(pltpu.make_async_copy(g, gs.at[d, into], sems.at[d, j, 1]))
        mine.append(pltpu.make_async_copy(win_ref.at[:, column(d)], wi.at[d], wsems.at[d, 0]))
        mine.append(pltpu.make_async_copy(wout_ref.at[:, column(d)], wo.at[d], wsems.at[d, 1]))
        copies.append(mine)
    tables = []
    for j in range(blocks):
        table = rows_of(pieces[j][0], tok)[2]
        tables.append(pltpu.make_async_copy(table, ps.at[j], psems.at[j]))
        tables[j].start()

    for copy in copies[0] + copies[1]:
        copy.start()
    last = (((1,), (1,)), ((), ()))
    for d in range(n_tp):
        for copy in copies[d]:
            copy.wait()
        for copy in copies[d + 2] if d + 2 < n_tp else ():
            copy.start()
        if d == n_tp - 2:
            added = [pltpu.make_async_copy(base[0], bi, bsems.at[0])]
            added.append(pltpu.make_async_copy(base[1], bo, bsems.at[1]))
            for copy in added:
                copy.start()
        x = xs[d]
        g = gs[d] * jnp.asarray(SHRINK, BF16)
        ab = lax.dot_general(wi[d], x, last, preferred_element_type=F32)
        h = lax.dot_general(wo[d], g, last, preferred_element_type=F32)
        if d == 0:
            acc[pl.ds(0, 2 * ffl)] = ab
            acc[pl.ds(2 * ffl, ffl)] = h
        else:
            acc[pl.ds(0, 2 * ffl)] += ab
            acc[pl.ds(2 * ffl, ffl)] += h
    scale = []
    for j in range(blocks):
        tables[j].wait()
        first = weights_row(ps.at[j], where_ref[1], tok)
        scale.append(first + weights_row(ps.at[j], where_ref[2], tok))
    scale = jnp.concatenate(scale, axis=1)
    a = acc[pl.ds(0, ffl)]
    b = acc[pl.ds(ffl, ffl)]
    named = scale > 0.0
    dh = acc[pl.ds(2 * ffl, ffl)] * (scale * (1.0 / SHRINK))
    sig = jax.nn.sigmoid(a)
    silu = a * sig
    da = dh * b * sig * (1.0 + a * (1.0 - sig))
    dadb_ref[pl.ds(0, ffl)] = jnp.where(named, da, 0.0).astype(BF16)
    dadb_ref[pl.ds(ffl, ffl)] = jnp.where(named, dh * silu, 0.0).astype(BF16)
    hid_ref[...] = jnp.where(named, (0.5 * scale) * (silu * b), 0.0).astype(BF16)
    tile = oi.shape[2]
    tiles = width // tile
    leaving = {}
    for k in range(n_tp * tiles):
        slot, d, cols = k % 2, k // tiles, pl.ds(k % tiles * tile, tile)
        start = (where_ref[0] ^ d) * width + k % tiles * tile
        here = pl.ds(pl.multiple_of(start, tile), tile)
        for copy in leaving.pop(k - 2, ()):
            copy.wait()
        gi = jnp.dot(dadb_ref[...], xs[d, :, cols], preferred_element_type=F32)
        go = 2.0 * jnp.dot(hid_ref[...], gs[d, :, cols], preferred_element_type=F32)
        for copy in added if k == 0 else ():
            copy.wait()
        oi[slot] = (gi + bi[:, here].astype(F32)).astype(BF16)
        oo[slot] = (go + bo[:, here].astype(F32)).astype(BF16)
        leaving[k] = (
            pltpu.make_async_copy(oi.at[slot], gin_ref.at[:, here], osems.at[slot, 0]),
            pltpu.make_async_copy(oo.at[slot], gout_ref.at[:, here], osems.at[slot, 1]),
        )
        for copy in leaving[k]:
            copy.start()
    for copies in leaving.values():
        for copy in copies:
            copy.wait()


def far_call(where, pieces, w_in, w_out, tok, base):
    n_tp = len(pieces[0])
    flat = [piece for block in pieces for piece in block]
    sizes = [len(piece) for piece in flat]
    arrays = [array for piece in flat for array in piece]
    blocks = len(pieces)
    rows, width = blocks * tok, arrays[0].shape[1]
    ffl, depth = w_out.shape
    tile = width
    hbm = pl.BlockSpec(memory_space=pltpu.HBM)
    return pl.pallas_call(
        functools.partial(far_kernel, n_tp, sizes),
        out_shape=[
            jax.ShapeDtypeStruct((2 * ffl, depth), BF16),
            jax.ShapeDtypeStruct((ffl, depth), BF16),
        ],
        in_specs=[pl.BlockSpec(memory_space=pltpu.SMEM)] + [hbm] * (4 + len(arrays)),
        out_specs=[hbm, hbm],
        scratch_shapes=[
            pltpu.VMEM((n_tp, rows, width), BF16),
            pltpu.VMEM((n_tp, rows, width), BF16),
            pltpu.VMEM((blocks, 16, width), BF16),
            pltpu.VMEM((n_tp, 2 * ffl, width), BF16),
            pltpu.VMEM((n_tp, ffl, width), BF16),
            pltpu.VMEM((3 * ffl, rows), F32),
            pltpu.VMEM((2 * ffl, rows), BF16),
            pltpu.VMEM((ffl, rows), BF16),
            pltpu.VMEM((2 * ffl, depth), BF16),
            pltpu.VMEM((ffl, depth), BF16),
            pltpu.VMEM((2, 2 * ffl, tile), BF16),
            pltpu.VMEM((2, ffl, tile), BF16),
            pltpu.SemaphoreType.DMA((n_tp, blocks, 2)),
            pltpu.SemaphoreType.DMA((blocks,)),
            pltpu.SemaphoreType.DMA((n_tp, 2)),
            pltpu.SemaphoreType.DMA((2,)),
            pltpu.SemaphoreType.DMA((2, 2)),
        ],
        compiler_params=pltpu.CompilerParams(vmem_limit_bytes=VMEM_LIMIT),
        cost_estimate=pl.CostEstimate(
            flops=12 * rows * ffl * depth,
            bytes_accessed=2 * (9 * ffl + 2 * rows) * depth,
            transcendentals=rows * ffl,
        ),
        name="far",
    )(where, w_in, w_out, *arrays, *base)


def grads_kernel(steps, sizes, added, filled, where_ref, dadb_ref, hid_ref, *refs):
    pieces = []
    tok = hid_ref.shape[1] * len(steps) // len(sizes)
    for size in sizes:
        pieces.append(rows_of(refs[:size], tok))
        refs = refs[size:]
    base, refs = (refs[:2], refs[2:]) if added else ((), refs)
    gin_ref, gout_ref, xs, gs, oi, oo, bi, bo, sems, bsems, osems = refs[2 if filled else 0 :]
    width = pieces[0][0].shape[1]
    slots, _, tile = xs.shape
    tiles = width // tile
    total = len(steps) * tiles

    def column(k):
        start = (where_ref[0] ^ steps[k // tiles]) * width + k % tiles * tile
        return pl.ds(pl.multiple_of(start, tile), tile)

    def fetch(k):
        slot, cols = k % slots, pl.ds(k % tiles * tile, tile)
        copies = []
        for i, (x, g, _) in enumerate(pieces[k // tiles :: len(steps)]):
            into = pl.ds(i * tok, tok)
            copies.append(pltpu.make_async_copy(x.at[:, cols], xs.at[slot, into], sems.at[slot, i, 0]))
            copies.append(pltpu.make_async_copy(g.at[:, cols], gs.at[slot, into], sems.at[slot, i, 1]))
        for i, (src, dst) in enumerate(zip(base, (bi, bo))):
            copies.append(pltpu.make_async_copy(src.at[:, column(k)], dst.at[slot], bsems.at[slot, i]))
        for copy in copies:
            copy.start()
        return copies

    coming = [fetch(k) for k in range(min(slots - 1, total))]
    leaving = {}
    for k in range(total):
        slot = k % slots
        if k + slots - 1 < total:
            coming.append(fetch(k + slots - 1))
        for copy in coming[k]:
            copy.wait()
        for copy in leaving.pop(k - slots, ()):
            copy.wait()
        gi = jnp.dot(dadb_ref[...], xs[slot], preferred_element_type=F32)
        go = 2.0 * jnp.dot(hid_ref[...], gs[slot], preferred_element_type=F32)
        if added:
            gi = gi + bi[slot].astype(F32)
            go = go + bo[slot].astype(F32)
        oi[slot] = gi.astype(BF16)
        oo[slot] = go.astype(BF16)
        leaving[k] = (
            pltpu.make_async_copy(oi.at[slot], gin_ref.at[:, column(k)], osems.at[slot, 0]),
            pltpu.make_async_copy(oo.at[slot], gout_ref.at[:, column(k)], osems.at[slot, 1]),
        )
        for copy in leaving[k]:
            copy.start()
    for copies in leaving.values():
        for copy in copies:
            copy.wait()


def grads_call(where, dadb, hid, pieces, steps, base=(), filled=()):
    n_tp = len(pieces[0])
    flat = [block[d] for block in pieces for d in steps]
    sizes = [len(piece) for piece in flat]
    arrays = [array for piece in flat for array in piece]
    width = arrays[0].shape[1]
    ffl, rows = hid.shape
    depth = n_tp * width
    tile = min(512, width)
    vmem = pl.BlockSpec(memory_space=pltpu.VMEM)
    hbm = pl.BlockSpec(memory_space=pltpu.HBM)
    operands = [where, dadb, hid, *arrays, *base, *filled]
    return pl.pallas_call(
        functools.partial(grads_kernel, steps, sizes, len(base) > 0, len(filled) > 0),
        out_shape=[
            jax.ShapeDtypeStruct((2 * ffl, depth), BF16),
            jax.ShapeDtypeStruct((ffl, depth), BF16),
        ],
        in_specs=[pl.BlockSpec(memory_space=pltpu.SMEM), vmem, vmem]
        + [hbm] * (len(operands) - 3),
        out_specs=[hbm, hbm],
        input_output_aliases={len(operands) - 2: 0, len(operands) - 1: 1} if filled else {},
        scratch_shapes=[
            pltpu.VMEM((SLOTS, rows, tile), BF16),
            pltpu.VMEM((SLOTS, rows, tile), BF16),
            pltpu.VMEM((SLOTS, 2 * ffl, tile), BF16),
            pltpu.VMEM((SLOTS, ffl, tile), BF16),
            pltpu.VMEM((SLOTS, 2 * ffl, tile), BF16),
            pltpu.VMEM((SLOTS, ffl, tile), BF16),
            pltpu.SemaphoreType.DMA((SLOTS, len(pieces), 2)),
            pltpu.SemaphoreType.DMA((SLOTS, 2)),
            pltpu.SemaphoreType.DMA((SLOTS, 2)),
        ],
        compiler_params=pltpu.CompilerParams(vmem_limit_bytes=VMEM_LIMIT),
        cost_estimate=pl.CostEstimate(
            flops=6 * rows * ffl * len(steps) * width,
            bytes_accessed=2 * (3 * ffl + 2 * rows) * len(steps) * width,
            transcendentals=0,
        ),
        name="grads",
    )(*operands)


def own_rows(tokens, out_grad, routes, probs, n_ep):
    tok, width = tokens.shape
    copies = jnp.arange(n_ep, dtype=jnp.int32)[:, None, None]
    table = jnp.sum(jnp.where(routes[None] == copies, probs[None], 0), axis=2).astype(BF16)
    table = table.reshape(n_ep * tok // width, width)
    table = jnp.pad(table, ((0, 16 - table.shape[0]), (0, 0)))
    return jnp.concatenate([tokens, out_grad, table])


def body(tokens, out_grad, routes, probs, w_in, w_out):
    n_ep, n_tp = lax.axis_size("ep"), lax.axis_size("tp")
    pairs = n_tp // 2
    ffl = w_out.shape[1]
    w_in = w_in.reshape(2 * ffl, w_in.shape[3])
    w_out = w_out[0]
    tok = tokens.shape[0]
    expert = lax.axis_index("ep") % (n_ep // 2)
    where = jnp.stack([lax.axis_index("tp"), expert, expert + n_ep // 2]).astype(jnp.int32)

    lanes = Lanes(1)
    have = {frozenset(): {2: own_rows(tokens, out_grad, routes, probs, n_ep)}}

    def held(name, part):
        parts = have[name]
        if part not in parts:
            if part == 2:
                parts[2] = jnp.concatenate([parts[0], parts[1]])
            else:
                parts[part] = parts[2][:tok] if part == 0 else parts[2][tok:]
        return parts[part]

    def arrays(name):
        parts = have[name]
        return (parts[2],) if 2 in parts else (parts[0], parts[1])

    names = [[name_of(e, y) for y in range(pairs)] for e in range(n_ep)]
    half_of = {name: 2 * e // n_ep for e in range(n_ep) for name in names[e]}
    missing = [n_ep * pairs - 2, n_ep * pairs]
    pieces = [None] * n_ep
    done = []
    terms = {}
    other = {frozenset(): (lanes.send(have[frozenset()][2], "t0"),)}
    plan = gather_plan(n_ep, n_tp)
    for target, bit, part, *first in plan:
        target = frozenset(target)
        before = []
        for what in first:
            before.append(done[what] if isinstance(what, int) else have[frozenset(what)][2])
        have.setdefault(target, {})[part] = lanes.send(held(target - {bit}, part), bit, *before)
        if 2 in have[target] or len(have[target]) == 2:
            other[target] = tuple(lanes.send(array, "t0") for array in arrays(target))
        half = half_of[target]
        missing[half] -= 2 if part == 2 else 1
        if missing[half]:
            continue
        blocks = range(half * n_ep // 2, (half + 1) * n_ep // 2)
        for e in blocks:
            pieces[e] = [
                arrays(names[e][d // 2]) if d % 2 == 0 else other[names[e][d // 2]]
                for d in range(n_tp)
            ]
        mine = pieces[blocks[0] : blocks[-1] + 1]
        if half == 0:
            out = rows_call(True, where, mine, w_in, w_out, tok)
            near = grads_call(where, out[0], out[1], mine, list(range(n_tp)))
            done += [out[1], hop(near[1][:16, :128], "tp", 1)]

    kept, leaving = out[2], out[3:]
    half_way = leaving[0].shape[0]
    for i, mine in enumerate(leaving):
        come = hop(mine, "tp", 1)
        total = kept[i * half_way : (i + 1) * half_way].astype(F32) + come.astype(F32)
        total = total.astype(BF16)
        for m in range(half_way):
            k = i * half_way + m
            terms[names[k // pairs][k % pairs]] = total[m]

    keep = {}
    for e in range(n_ep // 2):
        for y in range(pairs):
            keep[e, y] = terms[names[e][y]].astype(F32)
    top = n_ep // 4
    for e in range(n_ep // 2 - 1, top, -1):
        for y in range(pairs):
            if y and e > top:
                keep[e - top, y] += hop(keep[e, y].astype(BF16), "ep", top).astype(F32)
            elif e > top:
                keep[top, 0] += hop(keep[e, y].astype(BF16), "ep", e - top).astype(F32)
    for y in range(1, pairs):
        keep[top, 0] += hop(keep[top, y].astype(BF16), "tp", 2 * y).astype(F32)
    total = keep[0, 0]
    for e in range(top + 1):
        for y in range(pairs if e < top else 1):
            if e or y:
                sums = keep[e, y].astype(BF16)
                total = total + leap(sums, e, 2 * y).astype(F32)
    in_grad = total.astype(BF16)

    grad_in, grad_out = far_call(where, pieces[n_ep // 2 :], w_in, w_out, tok, near)
    return in_grad, grad_in.reshape(1, 2, ffl, -1), grad_out[None]


def solution(mesh):
    return jax.shard_map(
        body,
        mesh=mesh,
        in_specs=(
            P("ep", "tp"),
            P("ep", "tp"),
            P("ep", None),
            P("ep", None),
            P("ep", None, "tp", None),
            P("ep", "tp", None),
        ),
        out_specs=(P("ep", "tp"), P("ep", None, "tp", None), P("ep", "tp", None)),
        check_vma=False,
    )
```
